32 devices in a mesh: layer: 2 (over x), expert: 16 (over z, y, core).
Axes of the slice: x: 2, y: 2, z: 4, core: 2. Of those that a mesh axis runs over, the one named last changes fastest.
Arguments:
- weights: bfloat16 [16384, 7168], P(('layer', 'expert')), parts along dimension 0, may hold values from -6 to 6
- loadings: bfloat16 [16384, 256], P(('layer', 'expert')), parts along dimension 0, may hold values from -0.375 to 0.375
- bases: bfloat16 [128, 256, 7168], P('layer', 'expert'), parts along dimension 0, may hold values from -1.5 to 1.5
- coeff: float32 [8, 64], P('layer'), parts along dimension 0, may hold values from -2 to 2
Outputs:
- grad_a: float32 [16384, 256], P(('layer', 'expert')), parts along dimension 0
- grad_b: bfloat16 [128, 256, 7168], P('layer', 'expert'), parts along dimension 0
- grad_c: float32 [8, 64], P('layer'), parts along dimension 0
The draws below stay inside these ranges and needn't reach their ends.
There are 2 independent parts, one for each index of `layer`. The reference program is written for one: setup_inputs(seed, part) draws one part's arguments, and reference() takes and returns one part's arrays. A program takes and returns all parts, laid end to end along the dimension named above; each array names one. Nothing has to cross between parts.
All inputs are finite; a program needn't handle non-finite values.
Results may differ from the reference program's by a relative error of at most 0.0061.
Values may be sent and summed in bfloat16 or wider, within the bound.
No kernel may reach another device: no remote copies, remote signals or barrier semaphores. Data moves between devices by JAX's collectives and lax.ppermute only.
A program may use at most 128 MiB of HBM per device.

```python
import math
import jax
import jax.numpy as jnp
from jax import lax

D = 7168
FF = 2048
RANK = 256
K = 64
EXPERTS = 4


def block_levels(own_key, shape, pieces, least, largest):
    level, own = 1.0, jax.random.fold_in(own_key, 6)
    for axis_at, shards_of in pieces:
        draws = jnp.exp(jax.random.uniform(jax.random.fold_in(own, axis_at), (shards_of,), jnp.float32, least / len(pieces), largest / len(pieces)))
        level = level * jnp.repeat(draws, shape[axis_at] // shards_of).reshape([-1 if axis == axis_at else 1 for axis in range(len(shape))])
    return level


def scatter_about(stream_key, extent, deviation, bound, pieces=(), dtype=jnp.bfloat16):
    entries = jax.random.normal(stream_key, extent, jnp.float32) * deviation
    if len(pieces) > 0:
        entries = block_levels(stream_key, extent, pieces, -0.22, 0.18) * entries
    return jnp.clip(entries, min=-bound, max=bound).astype(dtype)


def setup_inputs(seed: int = 0, part: int = 0) -> dict:
    splits = jax.random.split(jax.random.key(seed), 5)
    own_keys = jax.random.split(jax.random.fold_in(splits[4], part), 5)
    weights = scatter_about(own_keys[0], (EXPERTS * FF, D), 1.0, 6.0, ((0, 16),))
    loadings = scatter_about(own_keys[1], (EXPERTS * FF, RANK), RANK ** -0.5, 0.375, ((0, 16),))
    bases = scatter_about(own_keys[2], (K, RANK, D), 0.25, 1.5, ((1, 16),))
    coeff = jnp.clip(jax.random.uniform(own_keys[3], (EXPERTS, K), jnp.float32, -2.0, 2.0), -2.0, 2.0)
    return {"weights": weights, "loadings": loadings, "bases": bases, "coeff": coeff}


def reference(weights, loadings, bases, coeff):
    mix_bf = jnp.tanh(coeff).astype(jnp.bfloat16)
    flat_bases = bases.reshape(K, RANK * D)
    weight_cube = weights.reshape(EXPERTS, FF, D)
    load_cube = loadings.reshape(EXPERTS, FF, RANK)

    def per_expert(items):
        weight_rows, load_rows, mix_row = items
        mixture = jnp.dot(mix_row[None, :], flat_bases, preferred_element_type=jnp.float32)
        mixture = mixture.astype(jnp.bfloat16).reshape(RANK, D)
        product = jnp.dot(load_rows, mixture, preferred_element_type=jnp.float32)
        residual = (product - weight_rows.astype(jnp.float32)).astype(jnp.bfloat16)
        grad_rows = lax.dot_general(residual, mixture, (((1,), (1,)), ((), ())), preferred_element_type=jnp.float32)
        grad_rows = grad_rows / math.sqrt(D)
        partial_value = lax.dot_general(load_rows, residual, (((0,), (0,)), ((), ())), preferred_element_type=jnp.float32)
        return (grad_rows, partial_value)
    grad_rows, partials = lax.map(per_expert, (weight_cube, load_cube, mix_bf))
    mix_full = mix_bf.astype(jnp.float32)
    grad_b = jnp.einsum('ek,erd->krd', mix_full, partials, precision=lax.Precision.HIGHEST)
    grad_b = (grad_b / math.sqrt(EXPERTS)).astype(jnp.bfloat16)
    basis_inner = jnp.einsum('krd,erd->ek', bases.astype(jnp.float32), partials, precision=lax.Precision.HIGHEST)
    slope = 1.0 - jnp.tanh(coeff) ** 2
    grad_c = slope * basis_inner / math.sqrt(RANK * D)
    return (grad_rows.reshape(EXPERTS * FF, RANK), grad_b, grad_c)
```

```python
import functools
import math

import jax
import jax.numpy as jnp
from jax import lax
from jax.experimental import pallas as pl
from jax.experimental.pallas import tpu as pltpu
from jax.sharding import PartitionSpec as P

F32, BF16 = jnp.float32, jnp.bfloat16
HIGHEST = lax.Precision.HIGHEST
CHUNKS = 4
VMEM_LIMIT = 32 * 2**20


def iota(shape, dim):
    return lax.broadcasted_iota(jnp.int32, shape, dim)


def params():
    return pltpu.CompilerParams(vmem_limit_bytes=VMEM_LIMIT)


def cost(flops, bytes_accessed):
    return pl.CostEstimate(flops=flops, bytes_accessed=bytes_accessed, transcendentals=0)


def column_block(width):
    for block in (896, 512, 256, 128):
        if width % block == 0:
            return block
    return width


def spread_kernel(rows, place_ref, coeff_ref, spread_ref, spread_t_ref):
    experts, bases = coeff_ref.shape
    mix = jnp.tanh(coeff_ref[...]).astype(BF16).astype(F32)
    place = place_ref[0]
    tall = experts * rows
    wide = bases * rows
    owner = jnp.bitwise_xor(iota((tall, bases), 0) // rows, place)
    picked = jnp.zeros((tall, bases), F32)
    for e in range(experts):
        picked = jnp.where(owner == e, mix[e : e + 1, :], picked)
    widen = (iota((bases, wide), 1) // rows == iota((bases, wide), 0)).astype(BF16)
    spread = jnp.dot(picked.astype(BF16), widen, preferred_element_type=F32)
    same = iota((tall, wide), 0) % rows == iota((tall, wide), 1) % rows
    spread = jnp.where(same, spread, 0.0)
    spread_ref[...] = spread.astype(BF16)
    spread_t_ref[...] = spread.T.astype(BF16)


def mix_kernel(spread_ref, bases_ref, *out_refs):
    mixed = jnp.dot(spread_ref[...], bases_ref[...], preferred_element_type=F32)
    rows = mixed.shape[0] // len(out_refs)
    for j, out_ref in enumerate(out_refs):
        out_ref[...] = mixed[j * rows : (j + 1) * rows].astype(BF16)


def fit_kernel(first, load_ref, load_t_ref, weights_ref, m0, m1, m2, m3, *refs):
    if first:
        near_ref, far_ref, grad_ref = refs
    else:
        before_ref, near_ref, far_ref, grad_ref = refs
    mixture = jnp.concatenate([m0[...], m1[...], m2[...], m3[...]], axis=0)
    product = jnp.dot(load_ref[...], mixture, preferred_element_type=F32)
    residual = (product - weights_ref[...].astype(F32)).astype(BF16)
    grad = lax.dot_general(
        residual, mixture, (((1,), (1,)), ((), ())), preferred_element_type=F32
    )
    partial = jnp.dot(load_t_ref[...], residual, preferred_element_type=F32)
    half = partial.shape[0] // 2
    near_ref[...] = partial[:half]
    far_ref[...] = partial[half:].astype(BF16)

    @pl.when(pl.program_id(0) == 0)
    def _():
        if first:
            grad_ref[...] = grad
        else:
            grad_ref[...] = before_ref[...] + grad

    @pl.when(pl.program_id(0) > 0)
    def _():
        grad_ref[...] += grad


def chip_sum_kernel(near_ref, got_ref, keep_ref, send_ref):
    total = near_ref[...] + got_ref[...].astype(F32)
    half = total.shape[0] // 2
    keep_ref[...] = total[:half]
    send_ref[...] = total[half:].astype(BF16)


def plane_sum_kernel(keep_ref, got_ref, *out_refs):
    total = keep_ref[...] + got_ref[...].astype(F32)
    rows = total.shape[0] // len(out_refs)
    for j, out_ref in enumerate(out_refs):
        out_ref[...] = total[j * rows : (j + 1) * rows].astype(BF16)


def inner_kernel(rows, experts, place_ref, bases_ref, *refs):
    *sum_refs, inner_ref, acc_ref = refs
    summed = jnp.concatenate([ref[...] for ref in sum_refs], axis=0)
    step = lax.dot_general(
        summed, bases_ref[...], (((1,), (1,)), ((), ())), preferred_element_type=F32
    )

    @pl.when(pl.program_id(0) == 0)
    def _():
        acc_ref[...] = step

    @pl.when(pl.program_id(0) > 0)
    def _():
        acc_ref[...] += step

    @pl.when(pl.program_id(0) == pl.num_programs(0) - 1)
    def _():
        tall, wide = acc_ref.shape
        bases = wide // rows
        same = iota((tall, wide), 0) % rows == iota((tall, wide), 1) % rows
        kept = jnp.where(same, acc_ref[...], 0.0)
        owner = jnp.bitwise_xor(iota((experts, tall), 1) // rows, place_ref[0])
        gather = (owner == iota((experts, tall), 0)).astype(F32)
        narrow = (iota((wide, bases), 0) // rows == iota((wide, bases), 1)).astype(F32)
        by_expert = jnp.dot(gather, kept, precision=HIGHEST, preferred_element_type=F32)
        inner_ref[...] = jnp.dot(
            by_expert, narrow, precision=HIGHEST, preferred_element_type=F32
        )


def basis_kernel(scale, aliased, spread_t_ref, *refs):
    if aliased:
        _, *sum_refs, out_ref = refs
    else:
        *sum_refs, out_ref = refs
    summed = jnp.concatenate([ref[...] for ref in sum_refs], axis=0)
    grad = jnp.dot(spread_t_ref[...], summed, preferred_element_type=F32)
    out_ref[...] = (grad * scale).astype(BF16)


def whole_spec(shape):
    return pl.BlockSpec(shape, lambda s: (0,) * len(shape))


def column_spec(rows, block, start=0):
    return pl.BlockSpec((rows, block), lambda s: (0, start + s))


def per_device(weights, loadings, bases, coeff):
    devices = lax.axis_size("expert")
    num_bases, rows, width = bases.shape
    experts = coeff.shape[0]
    group = devices // experts
    assert group == 4 and experts & (experts - 1) == 0
    ff = loadings.shape[0]
    rank = rows * devices
    tall, wide = experts * rows, num_bases * rows
    split = rows % 16 == 0
    chunks = CHUNKS if experts <= 8 else 1
    chunk = width // chunks
    block = column_block(chunk)
    steps = chunk // block
    me = lax.axis_index("expert")
    place = (me // group).astype(jnp.int32).reshape(1)
    smem = pl.BlockSpec(memory_space=pltpu.SMEM)
    vmem = pl.BlockSpec(memory_space=pltpu.VMEM)

    def send(x, flip):
        return lax.ppermute(x, "expert", [(i, i ^ flip) for i in range(devices)])

    def pieces_of(x):
        return [x[j * rows : (j + 1) * rows] for j in range(experts)]

    flat = bases.reshape(wide, width)
    spread, spread_t = pl.pallas_call(
        functools.partial(spread_kernel, rows),
        out_shape=(
            jax.ShapeDtypeStruct((tall, wide), BF16),
            jax.ShapeDtypeStruct((wide, tall), BF16),
        ),
        in_specs=[smem, vmem],
        out_specs=(vmem, vmem),
        compiler_params=params(),
        name="spread",
    )(place, coeff)

    local = jnp.arange(rank, dtype=jnp.int32)
    piece = local // rows
    flips = (piece % experts) * group + (piece // experts % 2) * 2 + piece // (2 * experts)
    absolute = (me ^ flips) * rows + local % rows
    order = (jnp.arange(rank, dtype=jnp.int32)[:, None] == absolute[None, :]).astype(BF16)
    load = jnp.dot(loadings, order, preferred_element_type=F32).astype(BF16)
    load_t = lax.dot_general(
        order, loadings, (((0,), (1,)), ((), ())), preferred_element_type=F32
    ).astype(BF16)

    def mix_chunk(j):
        count = experts if split else 1
        outs = pl.pallas_call(
            mix_kernel,
            grid=(steps,),
            out_shape=[jax.ShapeDtypeStruct((tall // count, chunk), BF16)] * count,
            in_specs=[whole_spec((tall, wide)), column_spec(wide, block, j * steps)],
            out_specs=[column_spec(tall // count, block)] * count,
            compiler_params=params(),
            cost_estimate=cost(2 * tall * wide * chunk * 4, 2 * wide * chunk),
            name="mix",
        )(spread, flat)
        return list(outs) if split else pieces_of(outs[0])

    def fit_chunk(j, parts, before):
        first = before is None
        quarter = rank // 4
        extra = [] if first else [before]
        return pl.pallas_call(
            functools.partial(fit_kernel, first),
            grid=(steps,),
            out_shape=(
                jax.ShapeDtypeStruct((rank // 2, chunk), F32),
                jax.ShapeDtypeStruct((rank // 2, chunk), BF16),
                jax.ShapeDtypeStruct((ff, rank), F32),
            ),
            in_specs=[
                whole_spec((ff, rank)),
                whole_spec((rank, ff)),
                column_spec(ff, block, j * steps),
                *[column_spec(quarter, block)] * 4,
                *[whole_spec((ff, rank))] * len(extra),
            ],
            out_specs=(
                column_spec(rank // 2, block),
                column_spec(rank // 2, block),
                whole_spec((ff, rank)),
            ),
            compiler_params=params(),
            cost_estimate=cost(6 * ff * rank * chunk, 2 * ff * chunk),
            name="fit",
        )(load, load_t, weights, *parts, *extra)

    def chip_sum(near, got):
        half = rank // 4
        return pl.pallas_call(
            chip_sum_kernel,
            grid=(steps,),
            out_shape=(
                jax.ShapeDtypeStruct((half, chunk), F32),
                jax.ShapeDtypeStruct((half, chunk), BF16),
            ),
            in_specs=[column_spec(2 * half, block)] * 2,
            out_specs=(column_spec(half, block),) * 2,
            compiler_params=params(),
            cost_estimate=cost(2 * half * chunk, 16 * half * chunk),
            name="chip_sum",
        )(near, got)

    def plane_sum(keep, got):
        count = experts if split else 1
        outs = pl.pallas_call(
            plane_sum_kernel,
            grid=(steps,),
            out_shape=[jax.ShapeDtypeStruct((tall // count, chunk), BF16)] * count,
            in_specs=[column_spec(tall, block)] * 2,
            out_specs=[column_spec(tall // count, block)] * count,
            compiler_params=params(),
            cost_estimate=cost(tall * chunk, 8 * tall * chunk),
            name="plane_sum",
        )(keep, got)
        return list(outs) if split else pieces_of(outs[0])

    def sums_of(sums):
        return sums if split else [jnp.concatenate(sums, axis=0)]

    def inner_chunk(j, sums):
        sums = sums_of(sums)
        return pl.pallas_call(
            functools.partial(inner_kernel, rows, experts),
            grid=(steps,),
            out_shape=jax.ShapeDtypeStruct((experts, num_bases), F32),
            in_specs=[
                smem,
                column_spec(wide, block, j * steps),
                *[column_spec(tall // len(sums), block)] * len(sums),
            ],
            out_specs=whole_spec((experts, num_bases)),
            scratch_shapes=[pltpu.VMEM((tall, wide), F32)],
            compiler_params=params(),
            cost_estimate=cost(2 * tall * wide * chunk * 4, 2 * wide * chunk),
            name="inner",
        )(place, flat, *sums)

    def basis_chunk(j, sums, before):
        sums = sums_of(sums)
        aliased = before is not None
        extra = [before] if aliased else []
        return pl.pallas_call(
            functools.partial(basis_kernel, 1.0 / math.sqrt(experts), aliased),
            grid=(steps,),
            out_shape=jax.ShapeDtypeStruct((wide, width), BF16),
            in_specs=[
                whole_spec((wide, tall)),
                *[pl.BlockSpec(memory_space=pl.ANY)] * len(extra),
                *[column_spec(tall // len(sums), block)] * len(sums),
            ],
            out_specs=column_spec(wide, block, j * steps),
            input_output_aliases={1: 0} if aliased else {},
            compiler_params=params(),
            cost_estimate=cost(2 * tall * wide * chunk * 4, 2 * wide * chunk),
            name="basis",
        )(spread_t, *extra, *sums)

    grad_local, grad_flat, inners = None, None, []
    gathered = []
    for j in range(chunks):
        mixed = mix_chunk(j)
        got = [mixed[0]] + [send(mixed[k], k * group) for k in range(1, experts)]
        own = jnp.concatenate(got, axis=0)
        row = send(own, 2)
        gathered.append((own, row, send(own, 1), send(row, 1)))
    returned = []
    for j in range(chunks):
        near, far, grad_local = fit_chunk(j, gathered[j], grad_local)
        keep, away = chip_sum(near, send(far, 1))
        sums = plane_sum(keep, send(away, 2))
        returned.append([sums[0]] + [send(sums[k], k * group) for k in range(1, experts)])
    for j in range(chunks):
        inners.append(inner_chunk(j, returned[j]))
        grad_flat = basis_chunk(j, returned[j], grad_flat)

    grad_a = jnp.dot(
        grad_local, order.astype(F32).T, precision=HIGHEST, preferred_element_type=F32
    ) / math.sqrt(width)

    total = sum(inners[1:], inners[0])
    flip = 1
    while flip < devices:
        if flip * 2 < devices:
            a, b, c = (send(total, flip * k) for k in (1, 2, 3))
            total = (total + a) + (b + c)
            flip *= 4
        else:
            total = total + send(total, flip)
            flip *= 2
    slope = 1.0 - jnp.tanh(coeff) ** 2
    grad_c = slope * total / math.sqrt(rank * width)
    return (grad_a, grad_flat.reshape(num_bases, rows, width), grad_c)


def solution(mesh):
    in_specs = (
        P(("layer", "expert"), None),
        P(("layer", "expert"), None),
        P("layer", "expert", None),
        P("layer", None),
    )
    out_specs = (P(("layer", "expert"), None), P("layer", "expert", None), P("layer", None))
    return jax.shard_map(
        per_device, mesh=mesh, in_specs=in_specs, out_specs=out_specs, check_vma=False
    )
```

```python
import functools
import math

import jax
import jax.numpy as jnp
from jax import lax
from jax.experimental import pallas as pl
from jax.experimental.pallas import tpu as pltpu
from jax.sharding import PartitionSpec as P

F32, BF16 = jnp.float32, jnp.bfloat16
HIGHEST = lax.Precision.HIGHEST
SHARES = (1, 1)
LAG = 1
FAR = 2
FLOPS = 0
VMEM_LIMIT = 24 * 2**20


def iota(shape, dim):
    return lax.broadcasted_iota(jnp.int32, shape, dim)


def spread_kernel(rows, scale, place_ref, coeff_ref, spread_ref, spread_t_ref):
    experts, bases = coeff_ref.shape
    mix = jnp.tanh(coeff_ref[...]).astype(BF16).astype(F32)
    place = place_ref[0]
    tall = experts * rows
    wide = bases * rows
    owner = jnp.bitwise_xor(iota((tall, bases), 0) // rows, place)
    picked = jnp.zeros((tall, bases), F32)
    for e in range(experts):
        picked = jnp.where(owner == e, mix[e : e + 1, :], picked)
    widen = (iota((bases, wide), 1) // rows == iota((bases, wide), 0)).astype(BF16)
    spread = jnp.dot(picked.astype(BF16), widen, preferred_element_type=F32)
    same = iota((tall, wide), 0) % rows == iota((tall, wide), 1) % rows
    spread = jnp.where(same, spread, 0.0)
    spread_ref[...] = spread.astype(BF16)
    spread_t_ref[...] = (spread.T * scale).astype(BF16)


def streamed(start, source_ref, held_ref, sems):
    step = pl.program_id(0)
    block = held_ref.shape[2]

    def copy(at):
        column = start + at * block
        if not isinstance(column, int):
            column = pl.multiple_of(column, 128)
        return pltpu.make_async_copy(
            source_ref.at[:, pl.ds(column, block)], held_ref.at[at], sems.at[at]
        )

    @pl.when(step == 0)
    def _():
        for at in range(held_ref.shape[0]):
            copy(at).start()

    copy(step).wait()
    return held_ref[step]


def mix_kernel(start, spread_ref, bases_ref, *refs):
    *out_refs, held_ref, sems = refs
    held = streamed(start, bases_ref, held_ref, sems)
    mixed = jnp.dot(spread_ref[...], held, preferred_element_type=F32)
    rows = mixed.shape[0] // len(out_refs)
    for j, out_ref in enumerate(out_refs):
        out_ref[...] = mixed[j * rows : (j + 1) * rows].astype(BF16)


def join_kernel(*refs):
    *part_refs, out_ref = refs
    rows = part_refs[0].shape[0]
    for j, part_ref in enumerate(part_refs):
        out_ref[j * rows : (j + 1) * rows, :] = part_ref[...]


def fit_kernel(first, start, load_ref, load_t_ref, weights_ref, *refs):
    mixture_refs, refs = refs[:4], refs[4:]
    *refs, held_ref, sems = refs
    weights = streamed(start, weights_ref, held_ref, sems)
    if first:
        near_ref, *far_refs, grad_ref = refs
    else:
        before_ref, near_ref, *far_refs, grad_ref = refs
    mixture = jnp.concatenate([ref[...] for ref in mixture_refs], axis=0)
    product = jnp.dot(load_ref[...], mixture, preferred_element_type=F32)
    residual = (product - weights.astype(F32)).astype(BF16)
    grad = lax.dot_general(
        residual, mixture, (((1,), (1,)), ((), ())), preferred_element_type=F32
    )
    partial = jnp.dot(load_t_ref[...], residual, preferred_element_type=F32)
    half = partial.shape[0] // 2
    near_ref[...] = partial[:half]
    share = half // len(far_refs)
    for j, far_ref in enumerate(far_refs):
        far_ref[...] = partial[half + j * share : half + (j + 1) * share].astype(BF16)

    @pl.when(pl.program_id(0) == 0)
    def _():
        if first:
            grad_ref[...] = grad
        else:
            grad_ref[...] = before_ref[...] + grad

    @pl.when(pl.program_id(0) > 0)
    def _():
        grad_ref[...] += grad


def chip_sum_kernel(near_ref, *refs):
    *got_refs, keep_ref, send_ref = refs
    got = jnp.concatenate([ref[...] for ref in got_refs], axis=0)
    total = near_ref[...] + got.astype(F32)
    half = total.shape[0] // 2
    keep_ref[...] = total[:half]
    send_ref[...] = total[half:].astype(BF16)


def plane_sum_kernel(keep_ref, got_ref, *out_refs):
    total = keep_ref[...] + got_ref[...].astype(F32)
    rows = total.shape[0] // len(out_refs)
    for j, out_ref in enumerate(out_refs):
        out_ref[...] = total[j * rows : (j + 1) * rows].astype(BF16)


def inner_kernel(rows, experts, start, place_ref, bases_ref, *refs):
    *sum_refs, inner_ref, acc_ref, held_ref, sems = refs
    held = streamed(start, bases_ref, held_ref, sems)
    summed = jnp.concatenate([ref[...] for ref in sum_refs], axis=0)
    step = lax.dot_general(
        summed, held, (((1,), (1,)), ((), ())), preferred_element_type=F32
    )

    @pl.when(pl.program_id(0) == 0)
    def _():
        acc_ref[...] = step

    @pl.when(pl.program_id(0) > 0)
    def _():
        acc_ref[...] += step

    @pl.when(pl.program_id(0) == pl.num_programs(0) - 1)
    def _():
        tall, wide = acc_ref.shape
        bases = wide // rows
        same = iota((tall, wide), 0) % rows == iota((tall, wide), 1) % rows
        kept = jnp.where(same, acc_ref[...], 0.0)
        owner = jnp.bitwise_xor(iota((experts, tall), 1) // rows, place_ref[0])
        gather = (owner == iota((experts, tall), 0)).astype(F32)
        narrow = (iota((wide, bases), 0) // rows == iota((wide, bases), 1)).astype(F32)
        by_expert = jnp.dot(gather, kept, precision=HIGHEST, preferred_element_type=F32)
        inner_ref[...] = jnp.dot(
            by_expert, narrow, precision=HIGHEST, preferred_element_type=F32
        )


def basis_kernel(scale, skip, spread_t_ref, *refs):
    *sum_refs, out_ref, token_ref = refs[skip:]
    token_ref[...] = jnp.zeros_like(token_ref)
    summed = jnp.concatenate([ref[...] for ref in sum_refs], axis=0)
    grad = jnp.dot(spread_t_ref[...], summed, preferred_element_type=F32)
    if scale != 1.0:
        grad = grad * scale
    out_ref[...] = grad.astype(BF16)


def whole_spec(shape):
    return pl.BlockSpec(shape, lambda s: (0,) * len(shape))


def column_spec(rows, block, start=0):
    return pl.BlockSpec((rows, block), lambda s: (0, start + s))


def per_device(weights, loadings, bases, coeff):
    devices = lax.axis_size("expert")
    num_bases, rows, width = bases.shape
    experts = coeff.shape[0]
    group = devices // experts
    assert group == 4 and experts & (experts - 1) == 0
    ff = loadings.shape[0]
    rank = rows * devices
    tall, wide = experts * rows, num_bases * rows
    split = rows % 16 == 0
    widths = [width * share // sum(SHARES) for share in SHARES] if experts <= 8 else [width]
    chunks = len(widths)
    starts = [sum(widths[:j]) for j in range(chunks)]
    block = math.gcd(*widths)
    while block > 1024 and block % 256 == 0:
        block //= 2
    me = lax.axis_index("expert")
    place = (me // group).astype(jnp.int32).reshape(1)
    smem = pl.BlockSpec(memory_space=pltpu.SMEM)
    vmem = pl.BlockSpec(memory_space=pltpu.VMEM)
    anywhere = pl.BlockSpec(memory_space=pl.ANY)
    hbm = pl.BlockSpec(memory_space=pltpu.HBM)

    def send(x, flip):
        return lax.ppermute(x, "expert", [(i, i ^ flip) for i in range(devices)])

    def pieces_of(x):
        return [x[j * rows : (j + 1) * rows] for j in range(experts)]

    def pinned(array, spec):
        return pltpu.with_memory_space_constraint(array, pltpu.HBM) if spec is hbm else array

    def call(kernel, name, ins, outs, grid=None, after=(), flops=0, bytes_accessed=0, alias=None, **kw):
        count, late = len(ins), len(after)

        def body(*refs):
            kernel(*refs[:count], *refs[count + late :])

        return pl.pallas_call(
            body,
            out_shape=[shape for shape, _ in outs],
            in_specs=[spec for _, spec in ins] + [anywhere] * late,
            out_specs=[spec for _, spec in outs],
            compiler_params=pltpu.CompilerParams(vmem_limit_bytes=VMEM_LIMIT),
            cost_estimate=pl.CostEstimate(
                flops=FLOPS * flops, bytes_accessed=FLOPS * bytes_accessed, transcendentals=0
            ),
            input_output_aliases=alias or {},
            name=name,
            **({} if grid is None else {"grid": grid}),
            **kw,
        )(*[pinned(array, spec) for array, spec in ins], *after)

    def shape(*dims, dtype=BF16):
        return jax.ShapeDtypeStruct(dims, dtype)

    def col(rows_in, start=0):
        return column_spec(rows_in, block, start // block)

    def held(j, rows_in):
        steps = widths[j] // block
        return [pltpu.VMEM((steps, rows_in, block), BF16), pltpu.SemaphoreType.DMA((steps,))]

    flat = bases.reshape(wide, width)
    root = math.isqrt(experts)
    exact = root * root == experts and root & (root - 1) == 0
    spread, spread_t = call(
        functools.partial(spread_kernel, rows, 1.0 / root if exact else 1.0),
        "spread",
        [(place, smem), (coeff, vmem)],
        [(shape(tall, wide), vmem), (shape(wide, tall), vmem)],
    )
    late_scale = 1.0 if exact else 1.0 / math.sqrt(experts)

    local = jnp.arange(rank, dtype=jnp.int32)
    piece = local // rows
    flips = (piece % experts) * group + (piece // experts % 2) * 2 + piece // (2 * experts)
    absolute = (me ^ flips) * rows + local % rows
    order = (jnp.arange(rank, dtype=jnp.int32)[:, None] == absolute[None, :]).astype(BF16)
    load = jnp.dot(loadings, order, preferred_element_type=F32).astype(BF16)
    load_t = lax.dot_general(
        order, loadings, (((0,), (1,)), ((), ())), preferred_element_type=F32
    ).astype(BF16)

    def mix_chunk(j, after):
        count = experts if split else 1
        outs = call(
            functools.partial(mix_kernel, starts[j]),
            "mix",
            [(spread, whole_spec((tall, wide))), (flat, hbm)],
            [(shape(tall // count, widths[j]), col(tall // count))] * count,
            (widths[j] // block,),
            after,
            2 * tall * wide * widths[j] * 4,
            2 * wide * widths[j],
            scratch_shapes=held(j, wide),
        )
        return list(outs) if split else pieces_of(outs[0])

    def join(j, parts, after):
        if not split:
            return jnp.concatenate(parts, axis=0)
        return call(
            join_kernel,
            "join",
            [(part, vmem) for part in parts],
            [(shape(tall, widths[j]), vmem)],
            after=after,
        )[0]

    def fit_chunk(j, parts, before, after):
        first = before is None
        extra = [] if first else [(before, whole_spec((ff, rank)))]
        half = rank // 2
        return call(
            functools.partial(fit_kernel, first, starts[j]),
            "fit",
            [
                (load, whole_spec((ff, rank))),
                (load_t, whole_spec((rank, ff))),
                (weights, hbm),
                *[(part, col(half // 2)) for part in parts],
                *extra,
            ],
            [
                (shape(half, widths[j], dtype=F32), col(half)),
                *[(shape(half // FAR, widths[j]), col(half // FAR))] * FAR,
                (shape(ff, rank, dtype=F32), whole_spec((ff, rank))),
            ],
            (widths[j] // block,),
            after,
            6 * ff * rank * widths[j],
            2 * ff * widths[j],
            scratch_shapes=held(j, ff),
        )

    def chip_sum(j, near, got, after):
        half = rank // 4
        return call(
            chip_sum_kernel,
            "chip_sum",
            [(near, col(2 * half)), *[(part, col(2 * half // FAR)) for part in got]],
            [
                (shape(half, widths[j], dtype=F32), col(half)),
                (shape(half, widths[j]), col(half)),
            ],
            (widths[j] // block,),
            after,
            2 * half * widths[j],
            16 * half * widths[j],
        )

    def plane_sum(j, keep, got, after):
        count = experts if split else 1
        outs = call(
            plane_sum_kernel,
            "plane_sum",
            [(keep, col(tall)), (got, col(tall))],
            [(shape(tall // count, widths[j]), col(tall // count))] * count,
            (widths[j] // block,),
            after,
            tall * widths[j],
            8 * tall * widths[j],
        )
        return list(outs) if split else pieces_of(outs[0])

    def sums_of(sums):
        sums = sums if split else [jnp.concatenate(sums, axis=0)]
        return [(part, col(tall // len(sums))) for part in sums]

    def inner_chunk(j, sums, after):
        return call(
            functools.partial(inner_kernel, rows, experts, starts[j]),
            "inner",
            [(place, smem), (flat, hbm), *sums_of(sums)],
            [(shape(experts, num_bases, dtype=F32), whole_spec((experts, num_bases)))],
            (widths[j] // block,),
            after,
            2 * tall * wide * widths[j] * 4,
            2 * wide * widths[j],
            scratch_shapes=[pltpu.VMEM((tall, wide), F32), *held(j, wide)],
        )[0]

    def basis_chunk(j, sums, before, after, first=0, last=None):
        extra = [] if before is None else [(before, hbm)]
        last = widths[j] // block if last is None else last
        size = (last - first) * block
        return call(
            functools.partial(basis_kernel, late_scale, len(extra)),
            "basis",
            [
                (spread_t, whole_spec((wide, tall))),
                *extra,
                *[(part, col(part.shape[0], first * block)) for part, _ in sums_of(sums)],
            ],
            [
                (shape(wide, width), col(wide, starts[j] + first * block)),
                (shape(8, 128, dtype=F32), whole_spec((8, 128))),
            ],
            (last - first,),
            after,
            2 * tall * wide * size * 4,
            2 * wide * size,
            alias={1: 0} if extra else None,
        )

    mixes, gathered, returned, inners = [], [], [], []
    for j in range(chunks):
        mixes.append(mix_chunk(j, [mixes[-1][0]] if j else []))
    done = [mixes[-1][0]]
    for j in range(chunks):
        mixed = mixes[j]
        got = [mixed[0]] + [send(mixed[k], k * group) for k in range(1, experts)]
        own = join(j, got, done)
        done = [own]
        row = send(own, 2)
        gathered.append((own, row, send(own, 1), send(row, 1)))
    grad_local, kept = None, {}

    def return_plane(j, after):
        keep, away = kept.pop(j)
        sums = plane_sum(j, keep, away, after)
        returned.append([sums[0]] + [send(sums[k], k * group) for k in range(1, experts)])
        return [sums[0]]

    for j in range(chunks):
        near, *far, grad_local = fit_chunk(j, gathered[j], grad_local, done)
        done = [near]
        if j >= LAG:
            done = return_plane(j - LAG, done)
        keep, away = chip_sum(j, near, [send(part, 1) for part in far], done)
        kept[j] = keep, send(away, 2)
        done = [keep]
    grad_a = jnp.dot(
        grad_local, order.astype(F32).T, precision=HIGHEST, preferred_element_type=F32
    ) / math.sqrt(width)
    for j in sorted(kept):
        done = return_plane(j, done + [pinned(grad_a, hbm)])
    grad_flat = None
    for j in range(chunks):
        inners.append(inner_chunk(j, returned[j], done))
        done = [inners[-1]]
        if j < chunks - 1:
            grad_flat, token = basis_chunk(j, returned[j], grad_flat, done)
            done = [token]

    total = sum(inners[1:], inners[0])
    flip, at, blocks = 1, 0, widths[-1] // block
    while flip < devices:
        upto = -(-(at + blocks) // 2) if at == 0 else blocks
        before = total
        if flip * 2 < devices:
            a, b, c = (send(total, flip * k) for k in (1, 2, 3))
            total = (total + a) + (b + c)
            flip *= 4
        else:
            total = total + send(total, flip)
            flip *= 2
        if at < upto:
            grad_flat, _ = basis_chunk(-1, returned[-1], grad_flat, [before], at, upto)
            at = upto
    slope = 1.0 - jnp.tanh(coeff) ** 2
    grad_c = slope * total / math.sqrt(rank * width)
    return (grad_a, grad_flat.reshape(num_bases, rows, width), grad_c)


def solution(mesh):
    in_specs = (
        P(("layer", "expert"), None),
        P(("layer", "expert"), None),
        P("layer", "expert", None),
        P("layer", None),
    )
    out_specs = (P(("layer", "expert"), None), P("layer", "expert", None), P("layer", None))
    return jax.shard_map(
        per_device, mesh=mesh, in_specs=in_specs, out_specs=out_specs, check_vma=False
    )
```

```python
import functools
import math

import jax
import jax.numpy as jnp
from jax import lax
from jax.experimental import pallas as pl
from jax.experimental.pallas import tpu as pltpu
from jax.sharding import PartitionSpec as P

F32, BF16 = jnp.float32, jnp.bfloat16
HIGHEST = lax.Precision.HIGHEST
SHARES = (1, 1)
LAG = 1
FAR = (2, 4)
FB = (0, 1)
Z_ORDER = (3, 2, 1)
P_ORDER = (1, 2, 3)
FETCH_COST = 1
FLOPS = 0
VMEM_LIMIT = 14 * 2**20


def iota(shape, dim):
    return lax.broadcasted_iota(jnp.int32, shape, dim)


def far_first(count):
    order = [k + j for k in range(0, count, 4) for j in (*Z_ORDER, 0)]
    return [k for k in order if k < count]


def by_place(refs):
    order = far_first(len(refs))
    return [refs[order.index(k)] for k in range(len(refs))]


def spread_kernel(rows, scale, inner_scale, place_ref, coeff_ref, *refs):
    spread_ref, spread_t_ref, slope_ref = refs
    experts, bases = coeff_ref.shape
    mix = jnp.tanh(coeff_ref[...])
    slope_ref[...] = (1.0 - mix * mix) * inner_scale
    mix = mix.astype(BF16).astype(F32)
    place = place_ref[0]
    tall = experts * rows
    wide = bases * rows
    owner = jnp.bitwise_xor(iota((tall, bases), 0) // rows, place)
    picked = jnp.zeros((tall, bases), F32)
    for e in range(experts):
        picked = jnp.where(owner == e, mix[e : e + 1, :], picked)
    widen = (iota((bases, wide), 1) // rows == iota((bases, wide), 0)).astype(BF16)
    spread = jnp.dot(picked.astype(BF16), widen, preferred_element_type=F32)
    same = iota((tall, wide), 0) % rows == iota((tall, wide), 1) % rows
    spread = jnp.where(same, spread, 0.0)
    spread_ref[...] = spread.astype(BF16)
    spread_t_ref[...] = (spread.T * scale).astype(BF16)


def streamed(start, source_ref, held_ref, sems):
    step = pl.program_id(0)
    block = held_ref.shape[2]

    def copy(at):
        column = start + at * block
        if not isinstance(column, int):
            column = pl.multiple_of(column, 128)
        return pltpu.make_async_copy(
            source_ref.at[:, pl.ds(column, block)], held_ref.at[at], sems.at[at]
        )

    @pl.when(step == 0)
    def _():
        for at in range(held_ref.shape[0]):
            copy(at).start()

    copy(step).wait()
    return held_ref[step]


def fetch_kernel(start, source_ref, held_ref, token_ref, sems):
    block = held_ref.shape[2]
    copies = [
        pltpu.make_async_copy(
            source_ref.at[:, start + at * block : start + (at + 1) * block],
            held_ref.at[at],
            sems.at[at],
        )
        for at in range(held_ref.shape[0])
    ]
    for copy in copies:
        copy.start()
    token_ref[...] = jnp.zeros_like(token_ref)
    for copy in copies:
        copy.wait()


def mix_kernel(start, spread_ref, bases_ref, *refs):
    *out_refs, held_ref, sems = refs
    held = streamed(start, bases_ref, held_ref, sems)
    mixed = jnp.dot(spread_ref[...], held, preferred_element_type=F32)
    rows = mixed.shape[0] // len(out_refs)
    for j, out_ref in enumerate(out_refs):
        out_ref[...] = mixed[j * rows : (j + 1) * rows].astype(BF16)


def join_kernel(*refs):
    *part_refs, out_ref = refs
    rows = part_refs[0].shape[0]
    for j, part_ref in enumerate(by_place(part_refs)):
        out_ref[j * rows : (j + 1) * rows, :] = part_ref[...]


def fit_kernel(first, start, load_ref, load_t_ref, weights_ref, *refs):
    mixture_refs, refs = refs[:4], refs[4:]
    *refs, held_ref, sems = refs
    weights = streamed(start, weights_ref, held_ref, sems)
    if first:
        near_ref, *far_refs, grad_ref = refs
    else:
        before_ref, near_ref, *far_refs, grad_ref = refs
    mixture = jnp.concatenate([ref[...] for ref in mixture_refs], axis=0)
    product = jnp.dot(load_ref[...], mixture, preferred_element_type=F32)
    residual = (product - weights.astype(F32)).astype(BF16)
    grad = lax.dot_general(
        residual, mixture, (((1,), (1,)), ((), ())), preferred_element_type=F32
    )
    partial = jnp.dot(load_t_ref[...], residual, preferred_element_type=F32)
    half = partial.shape[0] // 2
    near_ref[...] = partial[:half]
    share = half // len(far_refs)
    for j, far_ref in enumerate(far_refs):
        far_ref[...] = partial[half + j * share : half + (j + 1) * share].astype(BF16)

    @pl.when(pl.program_id(0) == 0)
    def _():
        if first:
            grad_ref[...] = grad
        else:
            grad_ref[...] = before_ref[...] + grad

    @pl.when(pl.program_id(0) > 0)
    def _():
        grad_ref[...] += grad


def chip_sum_kernel(near_ref, *refs):
    *got_refs, keep_ref, send_ref = refs
    got = jnp.concatenate([ref[...] for ref in got_refs], axis=0)
    total = near_ref[...] + got.astype(F32)
    half = total.shape[0] // 2
    keep_ref[...] = total[:half]
    send_ref[...] = total[half:].astype(BF16)


def plane_sum_kernel(keep_ref, got_ref, *out_refs):
    total = keep_ref[...] + got_ref[...].astype(F32)
    rows = total.shape[0] // len(out_refs)
    for j, out_ref in enumerate(out_refs):
        out_ref[...] = total[j * rows : (j + 1) * rows].astype(BF16)


def inner_kernel(rows, experts, start, place_ref, bases_ref, *refs):
    if start is None:
        *sum_refs, inner_ref, acc_ref = refs
        held = bases_ref[0]
    else:
        *sum_refs, inner_ref, acc_ref, held_ref, sems = refs
        held = streamed(start, bases_ref, held_ref, sems)
    summed = jnp.concatenate([ref[...] for ref in by_place(sum_refs)], axis=0)
    step = lax.dot_general(
        summed, held, (((1,), (1,)), ((), ())), preferred_element_type=F32
    )

    @pl.when(pl.program_id(0) == 0)
    def _():
        acc_ref[...] = step

    @pl.when(pl.program_id(0) > 0)
    def _():
        acc_ref[...] += step

    @pl.when(pl.program_id(0) == pl.num_programs(0) - 1)
    def _():
        tall, wide = acc_ref.shape
        bases = wide // rows
        same = iota((tall, wide), 0) % rows == iota((tall, wide), 1) % rows
        kept = jnp.where(same, acc_ref[...], 0.0)
        owner = jnp.bitwise_xor(iota((experts, tall), 1) // rows, place_ref[0])
        gather = (owner == iota((experts, tall), 0)).astype(F32)
        narrow = (iota((wide, bases), 0) // rows == iota((wide, bases), 1)).astype(F32)
        by_expert = jnp.dot(gather, kept, precision=HIGHEST, preferred_element_type=F32)
        inner_ref[...] = jnp.dot(
            by_expert, narrow, precision=HIGHEST, preferred_element_type=F32
        )


def basis_kernel(scale, skip, spread_t_ref, *refs):
    *sum_refs, out_ref, token_ref = refs[skip:]
    token_ref[...] = jnp.zeros_like(token_ref)
    summed = jnp.concatenate([ref[...] for ref in by_place(sum_refs)], axis=0)
    grad = jnp.dot(spread_t_ref[...], summed, preferred_element_type=F32)
    if scale != 1.0:
        grad = grad * scale
    out_ref[...] = grad.astype(BF16)


def add_kernel(turns, scaled, *refs):
    *part_refs, out_ref = refs
    if scaled:
        *part_refs, slope_ref = part_refs
    part = {turn: ref[...] for turn, ref in zip((*turns, 0), part_refs)}
    total = part[0] + part[1]
    if len(turns) == 3:
        total = total + (part[2] + part[3])
    out_ref[...] = total * slope_ref[...] if scaled else total


def whole_spec(shape):
    return pl.BlockSpec(shape, lambda s: (0,) * len(shape))


def column_spec(rows, block, start=0):
    return pl.BlockSpec((rows, block), lambda s: (0, start + s))


def per_device(weights, loadings, bases, coeff):
    devices = lax.axis_size("expert")
    num_bases, rows, width = bases.shape
    experts = coeff.shape[0]
    group = devices // experts
    assert group == 4 and experts & (experts - 1) == 0
    ff = loadings.shape[0]
    rank = rows * devices
    tall, wide = experts * rows, num_bases * rows
    split = rows % 16 == 0
    widths = [width * share // sum(SHARES) for share in SHARES] if experts <= 8 else [width]
    chunks = len(widths)
    starts = [sum(widths[:j]) for j in range(chunks)]
    block = math.gcd(*widths)
    while block > 1024 and block % 256 == 0:
        block //= 2
    me = lax.axis_index("expert")
    place = (me // group).astype(jnp.int32).reshape(1)
    smem = pl.BlockSpec(memory_space=pltpu.SMEM)
    vmem = pl.BlockSpec(memory_space=pltpu.VMEM)
    anywhere = pl.BlockSpec(memory_space=pl.ANY)
    hbm = pl.BlockSpec(memory_space=pltpu.HBM)

    def send(x, flip):
        return lax.ppermute(x, "expert", [(i, i ^ flip) for i in range(devices)])

    def send_places(parts):
        sent = {k: send(parts[k], k * group) for k in far_first(experts) if k}
        return [parts[0]] + [sent[k] for k in range(1, experts)]

    def pieces_of(x):
        return [x[j * rows : (j + 1) * rows] for j in range(experts)]

    def pinned(array, spec):
        return pltpu.with_memory_space_constraint(array, pltpu.HBM) if spec is hbm else array

    def call(kernel, name, ins, outs, grid=None, after=(), flops=0, bytes_accessed=0, alias=None, **kw):
        count, late = len(ins), len(after)

        def body(*refs):
            kernel(*refs[:count], *refs[count + late :])

        return pl.pallas_call(
            body,
            out_shape=[shape for shape, _ in outs],
            in_specs=[spec for _, spec in ins] + [anywhere] * late,
            out_specs=[spec for _, spec in outs],
            compiler_params=pltpu.CompilerParams(vmem_limit_bytes=VMEM_LIMIT),
            cost_estimate=pl.CostEstimate(
                flops=flops, bytes_accessed=bytes_accessed, transcendentals=0
            ),
            input_output_aliases=alias or {},
            name=name,
            **({} if grid is None else {"grid": grid}),
            **kw,
        )(*[pinned(array, spec) for array, spec in ins], *after)

    def shape(*dims, dtype=BF16):
        return jax.ShapeDtypeStruct(dims, dtype)

    def col(rows_in, start=0):
        return column_spec(rows_in, block, start // block)

    def held(j, rows_in):
        steps = widths[j] // block
        return [pltpu.VMEM((steps, rows_in, block), BF16), pltpu.SemaphoreType.DMA((steps,))]

    flat = bases.reshape(wide, width)
    root = math.isqrt(experts)
    exact = root * root == experts and root & (root - 1) == 0
    spread, spread_t, slope = call(
        functools.partial(
            spread_kernel, rows, 1.0 / root if exact else 1.0, 1.0 / math.sqrt(rank * width)
        ),
        "spread",
        [(place, smem), (coeff, vmem)],
        [
            (shape(tall, wide), vmem),
            (shape(wide, tall), vmem),
            (shape(experts, num_bases, dtype=F32), vmem),
        ],
    )
    late_scale = 1.0 if exact else 1.0 / math.sqrt(experts)

    local = jnp.arange(rank, dtype=jnp.int32)
    piece = local // rows
    flips = (piece % experts) * group + (piece // experts % 2) * 2 + piece // (2 * experts)
    absolute = (me ^ flips) * rows + local % rows
    order = (jnp.arange(rank, dtype=jnp.int32)[:, None] == absolute[None, :]).astype(BF16)
    load = jnp.dot(loadings, order, preferred_element_type=F32).astype(BF16)
    load_t = lax.dot_general(
        order, loadings, (((0,), (1,)), ((), ())), preferred_element_type=F32
    ).astype(BF16)

    def mix_chunk(j, after):
        count = experts if split else 1
        outs = call(
            functools.partial(mix_kernel, starts[j]),
            "mix",
            [(spread, whole_spec((tall, wide))), (flat, hbm)],
            [(shape(tall // count, widths[j]), col(tall // count))] * count,
            (widths[j] // block,),
            after,
            FLOPS * 2 * tall * wide * widths[j],
            FLOPS * 2 * wide * widths[j],
            scratch_shapes=held(j, wide),
        )
        return list(outs) if split else pieces_of(outs[0])

    def join(j, parts, after):
        if not split:
            return jnp.concatenate(parts, axis=0)
        return call(
            join_kernel,
            "join",
            [(parts[k], vmem) for k in far_first(experts)],
            [(shape(tall, widths[j]), vmem)],
            after=after,
        )[0]

    def far_parts(j):
        return FAR[min(j, len(FAR) - 1)]

    def fetch(j, source, after):
        steps, rows_in = widths[j] // block, source.shape[0]
        return call(
            functools.partial(fetch_kernel, starts[j]),
            "fetch",
            [(source, hbm)],
            [(shape(steps, rows_in, block), vmem), (shape(8, 128, dtype=F32), vmem)],
            after=after,
            bytes_accessed=FETCH_COST * 4 * rows_in * widths[j],
            scratch_shapes=[pltpu.SemaphoreType.DMA((steps,))],
        )

    def fit_chunk(j, parts, before, after):
        first = before is None
        extra = [] if first else [(before, whole_spec((ff, rank)))]
        half = rank // 2
        return call(
            functools.partial(fit_kernel, first, starts[j]),
            "fit",
            [
                (load, whole_spec((ff, rank))),
                (load_t, whole_spec((rank, ff))),
                (weights, hbm),
                *[(part, col(half // 2)) for part in parts],
                *extra,
            ],
            [
                (shape(half, widths[j], dtype=F32), col(half)),
                *[(shape(half // far_parts(j), widths[j]), col(half // far_parts(j)))] * far_parts(j),
                (shape(ff, rank, dtype=F32), whole_spec((ff, rank))),
            ],
            (widths[j] // block,),
            after,
            FLOPS * 6 * ff * rank * widths[j],
            FLOPS * 2 * ff * widths[j],
            scratch_shapes=held(j, ff),
        )

    def chip_sum(j, near, got, after):
        half = rank // 4
        return call(
            chip_sum_kernel,
            "chip_sum",
            [(near, col(2 * half)), *[(part, col(2 * half // len(got))) for part in got]],
            [
                (shape(half, widths[j], dtype=F32), col(half)),
                (shape(half, widths[j]), col(half)),
            ],
            (widths[j] // block,),
            after,
            FLOPS * 2 * half * widths[j],
            FLOPS * 16 * half * widths[j],
        )

    def plane_sum(j, keep, got, after):
        count = experts if split else 1
        outs = call(
            plane_sum_kernel,
            "plane_sum",
            [(keep, col(tall)), (got, col(tall))],
            [(shape(tall // count, widths[j]), col(tall // count))] * count,
            (widths[j] // block,),
            after,
            FLOPS * tall * widths[j],
            FLOPS * 8 * tall * widths[j],
        )
        return list(outs) if split else pieces_of(outs[0])

    def sums_of(sums):
        sums = sums if split else [jnp.concatenate(sums, axis=0)]
        return [(sums[k], col(tall // len(sums))) for k in far_first(len(sums))]

    def inner_chunk(j, sums, after, fetched=None):
        there = fetched is not None
        return call(
            functools.partial(inner_kernel, rows, experts, None if there else starts[j]),
            "inner",
            [
                (place, smem),
                (fetched, pl.BlockSpec((1, wide, block), lambda s: (s, 0, 0)))
                if there
                else (flat, hbm),
                *sums_of(sums),
            ],
            [(shape(experts, num_bases, dtype=F32), whole_spec((experts, num_bases)))],
            (widths[j] // block,),
            after,
            FLOPS * 2 * tall * wide * widths[j],
            FLOPS * 2 * wide * widths[j],
            scratch_shapes=[pltpu.VMEM((tall, wide), F32), *([] if there else held(j, wide))],
        )[0]

    def basis_chunk(j, sums, before, after, first=0, last=None):
        extra = [] if before is None else [(before, hbm)]
        last = widths[j] // block if last is None else last
        size = (last - first) * block
        return call(
            functools.partial(basis_kernel, late_scale, len(extra)),
            "basis",
            [
                (spread_t, whole_spec((wide, tall))),
                *extra,
                *[(part, col(part.shape[0], first * block)) for part, _ in sums_of(sums)],
            ],
            [
                (shape(wide, width), col(wide, starts[j] + first * block)),
                (shape(8, 128, dtype=F32), whole_spec((8, 128))),
            ],
            (last - first,),
            after,
            FLOPS * 2 * tall * wide * size,
            FLOPS * 2 * wide * size,
            alias={1: 0} if extra else None,
        )

    mixes, gathered, returned, inners = [], [], [], []
    for j in range(chunks):
        mixes.append(mix_chunk(j, [mixes[-1][0]] if j else []))
    done = [mixes[-1][0]]
    for j in range(chunks):
        mixed = mixes[j]
        got = send_places(mixed)
        own = join(j, got, done)
        done = [own]
        row = send(own, 2)
        gathered.append((own, row, send(own, 1), send(row, 1)))
    grad_local, kept, at_hand = None, {}, {}

    def return_plane(j, after):
        if split and j in FB:
            at_hand[j], token = fetch(j, flat, after)
            after = [token]
        keep, away = kept.pop(j)
        sums = plane_sum(j, keep, away, after)
        returned.append(send_places(sums))
        return [sums[0]]

    for j in range(chunks):
        near, *far, grad_local = fit_chunk(j, gathered[j], grad_local, done)
        done = [near]
        keep, away = chip_sum(j, near, [send(part, 1) for part in far], done)
        kept[j] = keep, send(away, 2)
        done = [keep]
        if j >= LAG:
            done = return_plane(j - LAG, done)
    grad_a = jnp.dot(
        grad_local, order.astype(F32).T, precision=HIGHEST, preferred_element_type=F32
    ) / math.sqrt(width)
    for j in sorted(kept):
        done = return_plane(j, done + [pinned(grad_a, hbm)])
    grad_flat = None
    for j in range(chunks):
        inners.append(inner_chunk(j, returned[j], done, at_hand.get(j)))
        done = [inners[-1]]
        if j < chunks - 1:
            grad_flat, token = basis_chunk(j, returned[j], grad_flat, done)
            done = [token]

    total = sum(inners[1:], inners[0])
    flip, at, blocks = 1, 0, widths[-1] // block
    while flip < devices:
        upto = -(-blocks // 2) if at == 0 else blocks
        turns = P_ORDER if flip * 2 < devices else (1,)
        got = {turn: send(total, turn * flip) for turn in turns}
        flip *= len(turns) + 1
        if at < upto:
            grad_flat, token = basis_chunk(-1, returned[-1], grad_flat, [total], at, upto)
            at = upto
        last = flip >= devices
        total = call(
            functools.partial(add_kernel, turns, last),
            "add",
            [(got[turn], vmem) for turn in turns] + [(total, vmem)] + [(slope, vmem)] * last,
            [(shape(experts, num_bases, dtype=F32), vmem)],
            after=[token],
        )[0]
    return (grad_a, grad_flat.reshape(num_bases, rows, width), total)


def solution(mesh):
    in_specs = (
        P(("layer", "expert"), None),
        P(("layer", "expert"), None),
        P("layer", "expert", None),
        P("layer", None),
    )
    out_specs = (P(("layer", "expert"), None), P("layer", "expert", None), P("layer", None))
    return jax.shard_map(
        per_device, mesh=mesh, in_specs=in_specs, out_specs=out_specs, check_vma=False
    )
```

```python
import functools
import math

import jax
import jax.numpy as jnp
from jax import lax
from jax.experimental import pallas as pl
from jax.experimental.pallas import tpu as pltpu
from jax.sharding import PartitionSpec as P

F32, BF16 = jnp.float32, jnp.bfloat16
HIGHEST = lax.Precision.HIGHEST
SHARES = (1, 1)
LAG = 1
LARGE = 2048
FAR = (2, 4)
FB = (0, 1)
Z_ORDER = (3, 2, 1)
P_ORDER = (1, 2, 3)
FETCH_COST = 1
FLOPS = 0
VMEM_LIMIT = 26 * 2**20


def iota(shape, dim):
    return lax.broadcasted_iota(jnp.int32, shape, dim)


def far_first(count):
    order = [k + j for k in range(0, count, 4) for j in (*Z_ORDER, 0)]
    return [k for k in order if k < count]


def by_place(refs):
    order = far_first(len(refs))
    return [refs[order.index(k)] for k in range(len(refs))]


def spread_kernel(rows, scale, inner_scale, place_ref, coeff_ref, *refs):
    spread_ref, spread_t_ref, slope_ref = refs
    experts, bases = coeff_ref.shape
    mix = jnp.tanh(coeff_ref[...])
    slope_ref[...] = (1.0 - mix * mix) * inner_scale
    mix = mix.astype(BF16).astype(F32)
    place = place_ref[0]
    tall = experts * rows
    wide = bases * rows
    owner = jnp.bitwise_xor(iota((tall, bases), 0) // rows, place)
    picked = jnp.zeros((tall, bases), F32)
    for e in range(experts):
        picked = jnp.where(owner == e, mix[e : e + 1, :], picked)
    widen = (iota((bases, wide), 1) // rows == iota((bases, wide), 0)).astype(BF16)
    spread = jnp.dot(picked.astype(BF16), widen, preferred_element_type=F32)
    same = iota((tall, wide), 0) % rows == iota((tall, wide), 1) % rows
    spread = jnp.where(same, spread, 0.0)
    spread_ref[...] = spread.astype(BF16)
    spread_t_ref[...] = (spread.T * scale).astype(BF16)


def streamed(start, source_ref, held_ref, sems):
    step = pl.program_id(0)
    block = held_ref.shape[2]

    def copy(at):
        column = start + at * block
        if not isinstance(column, int):
            column = pl.multiple_of(column, 128)
        return pltpu.make_async_copy(
            source_ref.at[:, pl.ds(column, block)], held_ref.at[at], sems.at[at]
        )

    @pl.when(step == 0)
    def _():
        for at in range(held_ref.shape[0]):
            copy(at).start()

    copy(step).wait()
    return held_ref[step]


def fetch_kernel(start, source_ref, held_ref, token_ref, sems):
    block = held_ref.shape[2]
    copies = [
        pltpu.make_async_copy(
            source_ref.at[:, start + at * block : start + (at + 1) * block],
            held_ref.at[at],
            sems.at[at],
        )
        for at in range(held_ref.shape[0])
    ]
    for copy in copies:
        copy.start()
    token_ref[...] = jnp.zeros_like(token_ref)
    for copy in copies:
        copy.wait()


def mix_kernel(start, spread_ref, bases_ref, *refs):
    *out_refs, held_ref, sems = refs
    held = streamed(start, bases_ref, held_ref, sems)
    mixed = jnp.dot(spread_ref[...], held, preferred_element_type=F32)
    rows = mixed.shape[0] // len(out_refs)
    for j, out_ref in enumerate(out_refs):
        out_ref[...] = mixed[j * rows : (j + 1) * rows].astype(BF16)


def join_kernel(*refs):
    *part_refs, out_ref = refs
    rows = part_refs[0].shape[0]
    for j, part_ref in enumerate(by_place(part_refs)):
        out_ref[j * rows : (j + 1) * rows, :] = part_ref[...]


def fit_kernel(first, start, load_ref, load_t_ref, weights_ref, *refs):
    mixture_refs, refs = refs[:4], refs[4:]
    *refs, held_ref, sems = refs
    weights = streamed(start, weights_ref, held_ref, sems)
    if first:
        near_ref, *far_refs, grad_ref = refs
    else:
        before_ref, near_ref, *far_refs, grad_ref = refs
    mixture = jnp.concatenate([ref[...] for ref in mixture_refs], axis=0)
    product = jnp.dot(load_ref[...], mixture, preferred_element_type=F32)
    residual = (product - weights.astype(F32)).astype(BF16)
    grad = lax.dot_general(
        residual, mixture, (((1,), (1,)), ((), ())), preferred_element_type=F32
    )
    partial = jnp.dot(load_t_ref[...], residual, preferred_element_type=F32)
    half = partial.shape[0] // 2
    near_ref[...] = partial[:half]
    share = half // len(far_refs)
    for j, far_ref in enumerate(far_refs):
        far_ref[...] = partial[half + j * share : half + (j + 1) * share].astype(BF16)

    @pl.when(pl.program_id(0) == 0)
    def _():
        if first:
            grad_ref[...] = grad
        else:
            grad_ref[...] = before_ref[...] + grad

    @pl.when(pl.program_id(0) > 0)
    def _():
        grad_ref[...] += grad


def chip_sum_kernel(near_ref, *refs):
    *got_refs, keep_ref, send_ref = refs
    got = jnp.concatenate([ref[...] for ref in got_refs], axis=0)
    total = near_ref[...] + got.astype(F32)
    half = total.shape[0] // 2
    keep_ref[...] = total[:half]
    send_ref[...] = total[half:].astype(BF16)


def plane_sum_kernel(keep_ref, got_ref, *out_refs):
    total = keep_ref[...] + got_ref[...].astype(F32)
    rows = total.shape[0] // len(out_refs)
    for j, out_ref in enumerate(out_refs):
        out_ref[...] = total[j * rows : (j + 1) * rows].astype(BF16)


def inner_kernel(rows, experts, start, place_ref, bases_ref, *refs):
    if start is None:
        *sum_refs, inner_ref, acc_ref = refs
        held = bases_ref[0]
    else:
        *sum_refs, inner_ref, acc_ref, held_ref, sems = refs
        held = streamed(start, bases_ref, held_ref, sems)
    summed = jnp.concatenate([ref[...] for ref in by_place(sum_refs)], axis=0)
    step = lax.dot_general(
        summed, held, (((1,), (1,)), ((), ())), preferred_element_type=F32
    )

    @pl.when(pl.program_id(0) == 0)
    def _():
        acc_ref[...] = step

    @pl.when(pl.program_id(0) > 0)
    def _():
        acc_ref[...] += step

    @pl.when(pl.program_id(0) == pl.num_programs(0) - 1)
    def _():
        tall, wide = acc_ref.shape
        bases = wide // rows
        same = iota((tall, wide), 0) % rows == iota((tall, wide), 1) % rows
        kept = jnp.where(same, acc_ref[...], 0.0)
        owner = jnp.bitwise_xor(iota((experts, tall), 1) // rows, place_ref[0])
        gather = (owner == iota((experts, tall), 0)).astype(F32)
        narrow = (iota((wide, bases), 0) // rows == iota((wide, bases), 1)).astype(F32)
        by_expert = jnp.dot(gather, kept, precision=HIGHEST, preferred_element_type=F32)
        inner_ref[...] = jnp.dot(
            by_expert, narrow, precision=HIGHEST, preferred_element_type=F32
        )


def basis_kernel(scale, skip, spread_t_ref, *refs):
    *sum_refs, out_ref, token_ref = refs[skip:]
    token_ref[...] = jnp.zeros_like(token_ref)
    summed = jnp.concatenate([ref[...] for ref in by_place(sum_refs)], axis=0)
    grad = jnp.dot(spread_t_ref[...], summed, preferred_element_type=F32)
    if scale != 1.0:
        grad = grad * scale
    out_ref[...] = grad.astype(BF16)


def add_kernel(turns, scaled, *refs):
    *part_refs, out_ref = refs
    if scaled:
        *part_refs, slope_ref = part_refs
    part = {turn: ref[...] for turn, ref in zip((*turns, 0), part_refs)}
    total = part[0] + part[1]
    if len(turns) == 3:
        total = total + (part[2] + part[3])
    out_ref[...] = total * slope_ref[...] if scaled else total


def whole_spec(shape):
    return pl.BlockSpec(shape, lambda s: (0,) * len(shape))


def column_spec(rows, block, start=0):
    return pl.BlockSpec((rows, block), lambda s: (0, start + s))


def per_device(weights, loadings, bases, coeff):
    devices = lax.axis_size("expert")
    num_bases, rows, width = bases.shape
    experts = coeff.shape[0]
    group = devices // experts
    assert group == 4 and experts & (experts - 1) == 0
    ff = loadings.shape[0]
    rank = rows * devices
    tall, wide = experts * rows, num_bases * rows
    split = rows % 16 == 0
    widths = [width * share // sum(SHARES) for share in SHARES] if experts <= 8 else [width]
    chunks = len(widths)
    starts = [sum(widths[:j]) for j in range(chunks)]
    block = math.gcd(*widths)
    while block > LARGE and block % 256 == 0:
        block //= 2
    small = block // 2 if block % 256 == 0 else block
    me = lax.axis_index("expert")
    place = (me // group).astype(jnp.int32).reshape(1)
    smem = pl.BlockSpec(memory_space=pltpu.SMEM)
    vmem = pl.BlockSpec(memory_space=pltpu.VMEM)
    anywhere = pl.BlockSpec(memory_space=pl.ANY)
    hbm = pl.BlockSpec(memory_space=pltpu.HBM)

    def send(x, flip):
        return lax.ppermute(x, "expert", [(i, i ^ flip) for i in range(devices)])

    def send_places(parts):
        sent = {k: send(parts[k], k * group) for k in far_first(experts) if k}
        return [parts[0]] + [sent[k] for k in range(1, experts)]

    def pieces_of(x):
        return [x[j * rows : (j + 1) * rows] for j in range(experts)]

    def pinned(array, spec):
        return pltpu.with_memory_space_constraint(array, pltpu.HBM) if spec is hbm else array

    def call(kernel, name, ins, outs, grid=None, after=(), flops=0, bytes_accessed=0, alias=None, **kw):
        count, late = len(ins), len(after)

        def body(*refs):
            kernel(*refs[:count], *refs[count + late :])

        return pl.pallas_call(
            body,
            out_shape=[shape for shape, _ in outs],
            in_specs=[spec for _, spec in ins] + [anywhere] * late,
            out_specs=[spec for _, spec in outs],
            compiler_params=pltpu.CompilerParams(vmem_limit_bytes=VMEM_LIMIT),
            cost_estimate=pl.CostEstimate(
                flops=flops, bytes_accessed=bytes_accessed, transcendentals=0
            ),
            input_output_aliases=alias or {},
            name=name,
            **({} if grid is None else {"grid": grid}),
            **kw,
        )(*[pinned(array, spec) for array, spec in ins], *after)

    def shape(*dims, dtype=BF16):
        return jax.ShapeDtypeStruct(dims, dtype)

    def col(rows_in, start=0, size=None):
        size = size or block
        return column_spec(rows_in, size, start // size)

    def held(j, rows_in, size):
        steps = widths[j] // size
        return [pltpu.VMEM((steps, rows_in, size), BF16), pltpu.SemaphoreType.DMA((steps,))]

    flat = bases.reshape(wide, width)
    root = math.isqrt(experts)
    exact = root * root == experts and root & (root - 1) == 0
    spread, spread_t, slope = call(
        functools.partial(
            spread_kernel, rows, 1.0 / root if exact else 1.0, 1.0 / math.sqrt(rank * width)
        ),
        "spread",
        [(place, smem), (coeff, vmem)],
        [
            (shape(tall, wide), vmem),
            (shape(wide, tall), vmem),
            (shape(experts, num_bases, dtype=F32), vmem),
        ],
    )
    late_scale = 1.0 if exact else 1.0 / math.sqrt(experts)

    local = jnp.arange(rank, dtype=jnp.int32)
    piece = local // rows
    flips = (piece % experts) * group + (piece // experts % 2) * 2 + piece // (2 * experts)
    absolute = (me ^ flips) * rows + local % rows
    order = (jnp.arange(rank, dtype=jnp.int32)[:, None] == absolute[None, :]).astype(BF16)
    load = jnp.dot(loadings, order, preferred_element_type=F32).astype(BF16)
    load_t = lax.dot_general(
        order, loadings, (((0,), (1,)), ((), ())), preferred_element_type=F32
    ).astype(BF16)

    def mix_chunk(j, after):
        count = experts if split else 1
        outs = call(
            functools.partial(mix_kernel, starts[j]),
            "mix",
            [(spread, whole_spec((tall, wide))), (flat, hbm)],
            [(shape(tall // count, widths[j]), col(tall // count, 0, small))] * count,
            (widths[j] // small,),
            after,
            FLOPS * 2 * tall * wide * widths[j],
            FLOPS * 2 * wide * widths[j],
            scratch_shapes=held(j, wide, small),
        )
        return list(outs) if split else pieces_of(outs[0])

    def join(j, parts, after):
        if not split:
            return jnp.concatenate(parts, axis=0)
        return call(
            join_kernel,
            "join",
            [(parts[k], vmem) for k in far_first(experts)],
            [(shape(tall, widths[j]), vmem)],
            after=after,
        )[0]

    def far_parts(j):
        return FAR[min(j, len(FAR) - 1)]

    def fetch(j, source, after):
        steps, rows_in = widths[j] // block, source.shape[0]
        return call(
            functools.partial(fetch_kernel, starts[j]),
            "fetch",
            [(source, hbm)],
            [(shape(steps, rows_in, block), vmem), (shape(8, 128, dtype=F32), vmem)],
            after=after,
            bytes_accessed=FETCH_COST * 4 * rows_in * widths[j],
            scratch_shapes=[pltpu.SemaphoreType.DMA((steps,))],
        )

    def fit_chunk(j, parts, before, after):
        first = before is None
        extra = [] if first else [(before, whole_spec((ff, rank)))]
        half = rank // 2
        return call(
            functools.partial(fit_kernel, first, starts[j]),
            "fit",
            [
                (load, whole_spec((ff, rank))),
                (load_t, whole_spec((rank, ff))),
                (weights, hbm),
                *[(part, col(half // 2)) for part in parts],
                *extra,
            ],
            [
                (shape(half, widths[j], dtype=F32), col(half)),
                *[(shape(half // far_parts(j), widths[j]), col(half // far_parts(j)))] * far_parts(j),
                (shape(ff, rank, dtype=F32), whole_spec((ff, rank))),
            ],
            (widths[j] // block,),
            after,
            FLOPS * 6 * ff * rank * widths[j],
            FLOPS * 2 * ff * widths[j],
            scratch_shapes=held(j, ff, block),
        )

    def chip_sum(j, near, got, after):
        half = rank // 4
        return call(
            chip_sum_kernel,
            "chip_sum",
            [(near, col(2 * half)), *[(part, col(2 * half // len(got))) for part in got]],
            [
                (shape(half, widths[j], dtype=F32), col(half)),
                (shape(half, widths[j]), col(half)),
            ],
            (widths[j] // block,),
            after,
            FLOPS * 2 * half * widths[j],
            FLOPS * 16 * half * widths[j],
        )

    def plane_sum(j, keep, got, after):
        count = experts if split else 1
        outs = call(
            plane_sum_kernel,
            "plane_sum",
            [(keep, col(tall)), (got, col(tall))],
            [(shape(tall // count, widths[j]), col(tall // count))] * count,
            (widths[j] // block,),
            after,
            FLOPS * tall * widths[j],
            FLOPS * 8 * tall * widths[j],
        )
        return list(outs) if split else pieces_of(outs[0])

    def sums_of(sums):
        sums = sums if split else [jnp.concatenate(sums, axis=0)]
        return [(sums[k], col(tall // len(sums))) for k in far_first(len(sums))]

    def inner_chunk(j, sums, after, fetched=None):
        there = fetched is not None
        return call(
            functools.partial(inner_kernel, rows, experts, None if there else starts[j]),
            "inner",
            [
                (place, smem),
                (fetched, pl.BlockSpec((1, wide, block), lambda s: (s, 0, 0)))
                if there
                else (flat, hbm),
                *sums_of(sums),
            ],
            [(shape(experts, num_bases, dtype=F32), whole_spec((experts, num_bases)))],
            (widths[j] // block,),
            after,
            FLOPS * 2 * tall * wide * widths[j],
            FLOPS * 2 * wide * widths[j],
            scratch_shapes=[pltpu.VMEM((tall, wide), F32), *([] if there else held(j, wide, block))],
        )[0]

    def basis_chunk(j, sums, before, after, first=0, last=None):
        extra = [] if before is None else [(before, hbm)]
        unit = block if last is None else small
        last = widths[j] // block if last is None else last
        size = (last - first) * unit
        return call(
            functools.partial(basis_kernel, late_scale, len(extra)),
            "basis",
            [
                (spread_t, whole_spec((wide, tall))),
                *extra,
                *[(part, col(part.shape[0], first * unit, unit)) for part, _ in sums_of(sums)],
            ],
            [
                (shape(wide, width), col(wide, starts[j] + first * unit, unit)),
                (shape(8, 128, dtype=F32), whole_spec((8, 128))),
            ],
            (last - first,),
            after,
            FLOPS * 2 * tall * wide * size,
            FLOPS * 2 * wide * size,
            alias={1: 0} if extra else None,
        )

    mixes, gathered, returned, inners = [], [], [], []
    for j in range(chunks):
        mixes.append(mix_chunk(j, [mixes[-1][0]] if j else []))
    done = [mixes[-1][0]]
    for j in range(chunks):
        mixed = mixes[j]
        got = send_places(mixed)
        own = join(j, got, done)
        done = [own]
        row = send(own, 2)
        gathered.append((own, row, send(own, 1), send(row, 1)))
    grad_local, kept, at_hand = None, {}, {}

    def return_plane(j, after):
        if split and j in FB:
            at_hand[j], token = fetch(j, flat, after)
            after = [token]
        keep, away = kept.pop(j)
        sums = plane_sum(j, keep, away, after)
        returned.append(send_places(sums))
        return [sums[0]]

    for j in range(chunks):
        near, *far, grad_local = fit_chunk(j, gathered[j], grad_local, done)
        done = [near]
        keep, away = chip_sum(j, near, [send(part, 1) for part in far], done)
        kept[j] = keep, send(away, 2)
        done = [keep]
        if j >= LAG:
            done = return_plane(j - LAG, done)
    grad_a = jnp.dot(
        grad_local, order.astype(F32).T, precision=HIGHEST, preferred_element_type=F32
    ) / math.sqrt(width)
    for j in sorted(kept):
        done = return_plane(j, done + [pinned(grad_a, hbm)])
    grad_flat = None
    for j in range(chunks):
        inners.append(inner_chunk(j, returned[j], done, at_hand.get(j)))
        done = [inners[-1]]
        if j < chunks - 1:
            grad_flat, token = basis_chunk(j, returned[j], grad_flat, done)
            done = [token]

    total = sum(inners[1:], inners[0])
    flip, at, blocks = 1, 0, widths[-1] // small
    while flip < devices:
        upto = -(-blocks // 2) if at == 0 else blocks
        turns = P_ORDER if flip * 2 < devices else (1,)
        got = {turn: send(total, turn * flip) for turn in turns}
        flip *= len(turns) + 1
        if at < upto:
            grad_flat, token = basis_chunk(-1, returned[-1], grad_flat, [total], at, upto)
            at = upto
        last = flip >= devices
        total = call(
            functools.partial(add_kernel, turns, last),
            "add",
            [(got[turn], vmem) for turn in turns] + [(total, vmem)] + [(slope, vmem)] * last,
            [(shape(experts, num_bases, dtype=F32), vmem)],
            after=[token],
        )[0]
    return (grad_a, grad_flat.reshape(num_bases, rows, width), total)


def solution(mesh):
    in_specs = (
        P(("layer", "expert"), None),
        P(("layer", "expert"), None),
        P("layer", "expert", None),
        P("layer", None),
    )
    out_specs = (P(("layer", "expert"), None), P("layer", "expert", None), P("layer", None))
    return jax.shard_map(
        per_device, mesh=mesh, in_specs=in_specs, out_specs=out_specs, check_vma=False
    )
```

```python
import functools
import math

import jax
import jax.numpy as jnp
from jax import lax
from jax.experimental import pallas as pl
from jax.experimental.pallas import tpu as pltpu
from jax.sharding import PartitionSpec as P

F32, BF16 = jnp.float32, jnp.bfloat16
HIGHEST = lax.Precision.HIGHEST
SHARES = (1, 1)
LAG = 1
READY = (1, 2)
LARGE = 2048
FAR = (2, 4)
FB = (0, 1)
Z_ORDER = (3, 2, 1)
P_ORDER = (1, 2, 3)
FETCH_COST = 1
FLOPS = 0
VMEM_LIMIT = 26 * 2**20


def iota(shape, dim):
    return lax.broadcasted_iota(jnp.int32, shape, dim)


def far_first(count):
    order = [k + j for k in range(0, count, 4) for j in (*Z_ORDER, 0)]
    return [k for k in order if k < count]


def by_place(refs):
    order = far_first(len(refs))
    return [refs[order.index(k)] for k in range(len(refs))]


def spread_kernel(rows, scale, inner_scale, place_ref, coeff_ref, *refs):
    spread_ref, spread_t_ref, slope_ref = refs
    experts, bases = coeff_ref.shape
    mix = jnp.tanh(coeff_ref[...])
    slope_ref[...] = (1.0 - mix * mix) * inner_scale
    mix = mix.astype(BF16).astype(F32)
    place = place_ref[0]
    tall = experts * rows
    wide = bases * rows
    owner = jnp.bitwise_xor(iota((tall, bases), 0) // rows, place)
    picked = jnp.zeros((tall, bases), F32)
    for e in range(experts):
        picked = jnp.where(owner == e, mix[e : e + 1, :], picked)
    widen = (iota((bases, wide), 1) // rows == iota((bases, wide), 0)).astype(BF16)
    spread = jnp.dot(picked.astype(BF16), widen, preferred_element_type=F32)
    same = iota((tall, wide), 0) % rows == iota((tall, wide), 1) % rows
    spread = jnp.where(same, spread, 0.0)
    spread_ref[...] = spread.astype(BF16)
    spread_t_ref[...] = (spread.T * scale).astype(BF16)


def streamed(start, source_ref, held_ref, sems):
    step = pl.program_id(0)
    block = held_ref.shape[2]

    def copy(at):
        column = start + at * block
        if not isinstance(column, int):
            column = pl.multiple_of(column, 128)
        return pltpu.make_async_copy(
            source_ref.at[:, pl.ds(column, block)], held_ref.at[at], sems.at[at]
        )

    @pl.when(step == 0)
    def _():
        for at in range(held_ref.shape[0]):
            copy(at).start()

    copy(step).wait()
    return held_ref[step]


def fetch_kernel(start, source_ref, held_ref, token_ref, sems):
    block = held_ref.shape[2]
    copies = [
        pltpu.make_async_copy(
            source_ref.at[:, start + at * block : start + (at + 1) * block],
            held_ref.at[at],
            sems.at[at],
        )
        for at in range(held_ref.shape[0])
    ]
    for copy in copies:
        copy.start()
    token_ref[...] = jnp.zeros_like(token_ref)
    for copy in copies:
        copy.wait()


def mix_kernel(start, spread_ref, bases_ref, *refs):
    *out_refs, held_ref, sems = refs
    held = streamed(start, bases_ref, held_ref, sems)
    mixed = jnp.dot(spread_ref[...], held, preferred_element_type=F32)
    rows = mixed.shape[0] // len(out_refs)
    for j, out_ref in enumerate(out_refs):
        out_ref[...] = mixed[j * rows : (j + 1) * rows].astype(BF16)


def join_kernel(*refs):
    *part_refs, out_ref = refs
    rows = part_refs[0].shape[0]
    for j, part_ref in enumerate(by_place(part_refs)):
        out_ref[j * rows : (j + 1) * rows, :] = part_ref[...]


def fit_kernel(first, start, load_ref, load_t_ref, weights_ref, *refs):
    mixture_refs, refs = refs[:4], refs[4:]
    *refs, held_ref, sems = refs
    weights = streamed(start, weights_ref, held_ref, sems)
    if first:
        near_ref, *far_refs, grad_ref = refs
    else:
        before_ref, near_ref, *far_refs, grad_ref = refs
    mixture = jnp.concatenate([ref[...] for ref in mixture_refs], axis=0)
    product = jnp.dot(load_ref[...], mixture, preferred_element_type=F32)
    residual = (product - weights.astype(F32)).astype(BF16)
    grad = lax.dot_general(
        residual, mixture, (((1,), (1,)), ((), ())), preferred_element_type=F32
    )
    partial = jnp.dot(load_t_ref[...], residual, preferred_element_type=F32)
    half = partial.shape[0] // 2
    near_ref[...] = partial[:half]
    share = half // len(far_refs)
    for j, far_ref in enumerate(far_refs):
        far_ref[...] = partial[half + j * share : half + (j + 1) * share].astype(BF16)

    @pl.when(pl.program_id(0) == 0)
    def _():
        if first:
            grad_ref[...] = grad
        else:
            grad_ref[...] = before_ref[...] + grad

    @pl.when(pl.program_id(0) > 0)
    def _():
        grad_ref[...] += grad


def chip_sum_kernel(near_ref, *refs):
    *got_refs, keep_ref, send_ref = refs
    got = jnp.concatenate([ref[...] for ref in got_refs], axis=0)
    total = near_ref[...] + got.astype(F32)
    half = total.shape[0] // 2
    keep_ref[...] = total[:half]
    send_ref[...] = total[half:].astype(BF16)


def plane_sum_kernel(keep_ref, got_ref, *out_refs):
    total = keep_ref[...] + got_ref[...].astype(F32)
    rows = total.shape[0] // len(out_refs)
    for j, out_ref in enumerate(out_refs):
        out_ref[...] = total[j * rows : (j + 1) * rows].astype(BF16)


def inner_kernel(rows, experts, start, ready, steps, place_ref, bases_ref, *refs):
    if ready:
        ready_ref, *refs = refs
    if ready < steps:
        *refs, held_ref, sems = refs
    *sum_refs, inner_ref, acc_ref = refs
    summed = jnp.concatenate([ref[...] for ref in by_place(sum_refs)], axis=0)
    step = pl.program_id(0)

    def copy(at):
        block = held_ref.shape[2]
        column = start + at * block
        return pltpu.make_async_copy(
            bases_ref.at[:, column : column + block], held_ref.at[at - ready], sems.at[at - ready]
        )

    for at in range(steps):

        @pl.when(step == at)
        def _(at=at):
            if at == 0:
                for later in range(ready, steps):
                    copy(later).start()
            if at < ready:
                held = ready_ref[at]
            else:
                copy(at).wait()
                held = held_ref[at - ready]
            product = lax.dot_general(
                summed, held, (((1,), (1,)), ((), ())), preferred_element_type=F32
            )
            acc_ref[...] = product if at == 0 else acc_ref[...] + product

    @pl.when(pl.program_id(0) == pl.num_programs(0) - 1)
    def _():
        tall, wide = acc_ref.shape
        bases = wide // rows
        same = iota((tall, wide), 0) % rows == iota((tall, wide), 1) % rows
        kept = jnp.where(same, acc_ref[...], 0.0)
        owner = jnp.bitwise_xor(iota((experts, tall), 1) // rows, place_ref[0])
        gather = (owner == iota((experts, tall), 0)).astype(F32)
        narrow = (iota((wide, bases), 0) // rows == iota((wide, bases), 1)).astype(F32)
        by_expert = jnp.dot(gather, kept, precision=HIGHEST, preferred_element_type=F32)
        inner_ref[...] = jnp.dot(
            by_expert, narrow, precision=HIGHEST, preferred_element_type=F32
        )


def basis_kernel(scale, skip, spread_t_ref, *refs):
    *sum_refs, out_ref, token_ref = refs[skip:]
    token_ref[...] = jnp.zeros_like(token_ref)
    summed = jnp.concatenate([ref[...] for ref in by_place(sum_refs)], axis=0)
    grad = jnp.dot(spread_t_ref[...], summed, preferred_element_type=F32)
    if scale != 1.0:
        grad = grad * scale
    out_ref[...] = grad.astype(BF16)


def add_kernel(turns, scaled, *refs):
    *part_refs, out_ref = refs
    if scaled:
        *part_refs, slope_ref = part_refs
    part = {turn: ref[...] for turn, ref in zip((*turns, 0), part_refs)}
    total = part[0] + part[1]
    if len(turns) == 3:
        total = total + (part[2] + part[3])
    out_ref[...] = total * slope_ref[...] if scaled else total


def whole_spec(shape):
    return pl.BlockSpec(shape, lambda s: (0,) * len(shape))


def column_spec(rows, block, start=0):
    return pl.BlockSpec((rows, block), lambda s: (0, start + s))


def per_device(weights, loadings, bases, coeff):
    devices = lax.axis_size("expert")
    num_bases, rows, width = bases.shape
    experts = coeff.shape[0]
    group = devices // experts
    assert group == 4 and experts & (experts - 1) == 0
    ff = loadings.shape[0]
    rank = rows * devices
    tall, wide = experts * rows, num_bases * rows
    split = rows % 16 == 0
    widths = [width * share // sum(SHARES) for share in SHARES] if experts <= 8 else [width]
    chunks = len(widths)
    starts = [sum(widths[:j]) for j in range(chunks)]
    block = math.gcd(*widths)
    while block > LARGE and block % 256 == 0:
        block //= 2
    small = block // 2 if block % 256 == 0 else block
    me = lax.axis_index("expert")
    place = (me // group).astype(jnp.int32).reshape(1)
    smem = pl.BlockSpec(memory_space=pltpu.SMEM)
    vmem = pl.BlockSpec(memory_space=pltpu.VMEM)
    anywhere = pl.BlockSpec(memory_space=pl.ANY)
    hbm = pl.BlockSpec(memory_space=pltpu.HBM)

    def send(x, flip):
        return lax.ppermute(x, "expert", [(i, i ^ flip) for i in range(devices)])

    def send_places(parts):
        sent = {k: send(parts[k], k * group) for k in far_first(experts) if k}
        return [parts[0]] + [sent[k] for k in range(1, experts)]

    def pieces_of(x):
        return [x[j * rows : (j + 1) * rows] for j in range(experts)]

    def pinned(array, spec):
        return pltpu.with_memory_space_constraint(array, pltpu.HBM) if spec is hbm else array

    def call(kernel, name, ins, outs, grid=None, after=(), flops=0, bytes_accessed=0, alias=None, **kw):
        count, late = len(ins), len(after)

        def body(*refs):
            kernel(*refs[:count], *refs[count + late :])

        return pl.pallas_call(
            body,
            out_shape=[shape for shape, _ in outs],
            in_specs=[spec for _, spec in ins] + [anywhere] * late,
            out_specs=[spec for _, spec in outs],
            compiler_params=pltpu.CompilerParams(vmem_limit_bytes=VMEM_LIMIT),
            cost_estimate=pl.CostEstimate(
                flops=flops, bytes_accessed=bytes_accessed, transcendentals=0
            ),
            input_output_aliases=alias or {},
            name=name,
            **({} if grid is None else {"grid": grid}),
            **kw,
        )(*[pinned(array, spec) for array, spec in ins], *after)

    def shape(*dims, dtype=BF16):
        return jax.ShapeDtypeStruct(dims, dtype)

    def col(rows_in, start=0, size=None):
        size = size or block
        return column_spec(rows_in, size, start // size)

    def held(j, rows_in, size, ready=0):
        steps = widths[j] // size - ready
        if not steps:
            return []
        return [pltpu.VMEM((steps, rows_in, size), BF16), pltpu.SemaphoreType.DMA((steps,))]

    flat = bases.reshape(wide, width)
    root = math.isqrt(experts)
    exact = root * root == experts and root & (root - 1) == 0
    spread, spread_t, slope = call(
        functools.partial(
            spread_kernel, rows, 1.0 / root if exact else 1.0, 1.0 / math.sqrt(rank * width)
        ),
        "spread",
        [(place, smem), (coeff, vmem)],
        [
            (shape(tall, wide), vmem),
            (shape(wide, tall), vmem),
            (shape(experts, num_bases, dtype=F32), vmem),
        ],
    )
    late_scale = 1.0 if exact else 1.0 / math.sqrt(experts)

    local = jnp.arange(rank, dtype=jnp.int32)
    piece = local // rows
    flips = (piece % experts) * group + (piece // experts % 2) * 2 + piece // (2 * experts)
    absolute = (me ^ flips) * rows + local % rows
    order = (jnp.arange(rank, dtype=jnp.int32)[:, None] == absolute[None, :]).astype(BF16)
    load = jnp.dot(loadings, order, preferred_element_type=F32).astype(BF16)
    load_t = lax.dot_general(
        order, loadings, (((0,), (1,)), ((), ())), preferred_element_type=F32
    ).astype(BF16)

    def mix_chunk(j, after):
        count = experts if split else 1
        outs = call(
            functools.partial(mix_kernel, starts[j]),
            "mix",
            [(spread, whole_spec((tall, wide))), (flat, hbm)],
            [(shape(tall // count, widths[j]), col(tall // count, 0, small))] * count,
            (widths[j] // small,),
            after,
            FLOPS * 2 * tall * wide * widths[j],
            FLOPS * 2 * wide * widths[j],
            scratch_shapes=held(j, wide, small),
        )
        return list(outs) if split else pieces_of(outs[0])

    def join(j, parts, after):
        if not split:
            return jnp.concatenate(parts, axis=0)
        return call(
            join_kernel,
            "join",
            [(parts[k], vmem) for k in far_first(experts)],
            [(shape(tall, widths[j]), vmem)],
            after=after,
        )[0]

    def far_parts(j):
        return FAR[min(j, len(FAR) - 1)]

    def fetch(j, source, after):
        steps, rows_in = min(READY[j], widths[j] // block), source.shape[0]
        return call(
            functools.partial(fetch_kernel, starts[j]),
            "fetch",
            [(source, hbm)],
            [(shape(steps, rows_in, block), vmem), (shape(8, 128, dtype=F32), vmem)],
            after=after,
            bytes_accessed=FETCH_COST * 4 * rows_in * block * steps,
            scratch_shapes=[pltpu.SemaphoreType.DMA((steps,))],
        )

    def fit_chunk(j, parts, before, after):
        first = before is None
        extra = [] if first else [(before, whole_spec((ff, rank)))]
        half = rank // 2
        return call(
            functools.partial(fit_kernel, first, starts[j]),
            "fit",
            [
                (load, whole_spec((ff, rank))),
                (load_t, whole_spec((rank, ff))),
                (weights, hbm),
                *[(part, col(half // 2)) for part in parts],
                *extra,
            ],
            [
                (shape(half, widths[j], dtype=F32), col(half)),
                *[(shape(half // far_parts(j), widths[j]), col(half // far_parts(j)))] * far_parts(j),
                (shape(ff, rank, dtype=F32), whole_spec((ff, rank))),
            ],
            (widths[j] // block,),
            after,
            FLOPS * 6 * ff * rank * widths[j],
            FLOPS * 2 * ff * widths[j],
            scratch_shapes=held(j, ff, block),
        )

    def chip_sum(j, near, got, after):
        half = rank // 4
        return call(
            chip_sum_kernel,
            "chip_sum",
            [(near, col(2 * half)), *[(part, col(2 * half // len(got))) for part in got]],
            [
                (shape(half, widths[j], dtype=F32), col(half)),
                (shape(half, widths[j]), col(half)),
            ],
            (widths[j] // block,),
            after,
            FLOPS * 2 * half * widths[j],
            FLOPS * 16 * half * widths[j],
        )

    def plane_sum(j, keep, got, after):
        count = experts if split else 1
        outs = call(
            plane_sum_kernel,
            "plane_sum",
            [(keep, col(tall)), (got, col(tall))],
            [(shape(tall // count, widths[j]), col(tall // count))] * count,
            (widths[j] // block,),
            after,
            FLOPS * tall * widths[j],
            FLOPS * 8 * tall * widths[j],
        )
        return list(outs) if split else pieces_of(outs[0])

    def sums_of(sums):
        sums = sums if split else [jnp.concatenate(sums, axis=0)]
        return [(sums[k], col(tall // len(sums))) for k in far_first(len(sums))]

    def inner_chunk(j, sums, after, fetched=None):
        ready = 0 if fetched is None else fetched.shape[0]
        return call(
            functools.partial(inner_kernel, rows, experts, starts[j], ready, widths[j] // block),
            "inner",
            [
                (place, smem),
                (flat, hbm),
                *([(fetched, vmem)] if ready else []),
                *sums_of(sums),
            ],
            [(shape(experts, num_bases, dtype=F32), whole_spec((experts, num_bases)))],
            (widths[j] // block,),
            after,
            FLOPS * 2 * tall * wide * widths[j],
            FLOPS * 2 * wide * widths[j],
            scratch_shapes=[pltpu.VMEM((tall, wide), F32), *held(j, wide, block, ready)],
        )[0]

    def basis_chunk(j, sums, before, after, first=0, last=None):
        extra = [] if before is None else [(before, hbm)]
        unit = block if last is None else small
        last = widths[j] // block if last is None else last
        size = (last - first) * unit
        return call(
            functools.partial(basis_kernel, late_scale, len(extra)),
            "basis",
            [
                (spread_t, whole_spec((wide, tall))),
                *extra,
                *[(part, col(part.shape[0], first * unit, unit)) for part, _ in sums_of(sums)],
            ],
            [
                (shape(wide, width), col(wide, starts[j] + first * unit, unit)),
                (shape(8, 128, dtype=F32), whole_spec((8, 128))),
            ],
            (last - first,),
            after,
            FLOPS * 2 * tall * wide * size,
            FLOPS * 2 * wide * size,
            alias={1: 0} if extra else None,
        )

    mixes, gathered, returned, inners = [], [], [], []
    for j in range(chunks):
        mixes.append(mix_chunk(j, [mixes[-1][0]] if j else []))
    done = [mixes[-1][0]]
    for j in range(chunks):
        mixed = mixes[j]
        got = send_places(mixed)
        own = join(j, got, done)
        done = [own]
        row = send(own, 2)
        gathered.append((own, row, send(own, 1), send(row, 1)))
    grad_local, kept, at_hand = None, {}, {}

    def return_plane(j, after):
        if split and j in FB:
            at_hand[j], token = fetch(j, flat, after)
            after = [token]
        keep, away = kept.pop(j)
        sums = plane_sum(j, keep, away, after)
        returned.append(send_places(sums))
        return [sums[0]]

    for j in range(chunks):
        near, *far, grad_local = fit_chunk(j, gathered[j], grad_local, done)
        done = [near]
        keep, away = chip_sum(j, near, [send(part, 1) for part in far], done)
        kept[j] = keep, send(away, 2)
        done = [keep]
        if j >= LAG:
            done = return_plane(j - LAG, done)
    grad_a = jnp.dot(
        grad_local, order.astype(F32).T, precision=HIGHEST, preferred_element_type=F32
    ) / math.sqrt(width)
    for j in sorted(kept):
        done = return_plane(j, done + [pinned(grad_a, hbm)])
    grad_flat = None
    for j in range(chunks):
        inners.append(inner_chunk(j, returned[j], done, at_hand.get(j)))
        done = [inners[-1]]
        if j < chunks - 1:
            grad_flat, token = basis_chunk(j, returned[j], grad_flat, done)
            done = [token]

    total = sum(inners[1:], inners[0])
    flip, at, blocks = 1, 0, widths[-1] // small
    while flip < devices:
        upto = -(-blocks // 2) if at == 0 else blocks
        turns = P_ORDER if flip * 2 < devices else (1,)
        got = {turn: send(total, turn * flip) for turn in turns}
        flip *= len(turns) + 1
        if at < upto:
            grad_flat, token = basis_chunk(-1, returned[-1], grad_flat, [total], at, upto)
            at = upto
        last = flip >= devices
        total = call(
            functools.partial(add_kernel, turns, last),
            "add",
            [(got[turn], vmem) for turn in turns] + [(total, vmem)] + [(slope, vmem)] * last,
            [(shape(experts, num_bases, dtype=F32), vmem)],
            after=[token],
        )[0]
    return (grad_a, grad_flat.reshape(num_bases, rows, width), total)


def solution(mesh):
    in_specs = (
        P(("layer", "expert"), None),
        P(("layer", "expert"), None),
        P("layer", "expert", None),
        P("layer", None),
    )
    out_specs = (P(("layer", "expert"), None), P("layer", "expert", None), P("layer", None))
    return jax.shard_map(
        per_device, mesh=mesh, in_specs=in_specs, out_specs=out_specs, check_vma=False
    )
```

```python
import functools
import math

import jax
import jax.numpy as jnp
from jax import lax
from jax.experimental import pallas as pl
from jax.experimental.pallas import tpu as pltpu
from jax.sharding import PartitionSpec as P

F32, BF16 = jnp.float32, jnp.bfloat16
HIGHEST = lax.Precision.HIGHEST
SHARES = (1, 1)
LAG = 1
READY = (1, 2)
LARGE = 2048
FAR = (2, 4)
FB = (0, 1)
Z_ORDER = (3, 2, 1)
P_ORDER = (1, 2, 3)
FETCH_COST = 1
FLOPS = 0
VMEM_LIMIT = 20 * 2**20


def iota(shape, dim):
    return lax.broadcasted_iota(jnp.int32, shape, dim)


def far_first(count):
    order = [k + j for k in range(0, count, 4) for j in (*Z_ORDER, 0)]
    return [k for k in order if k < count]


def by_place(refs):
    order = far_first(len(refs))
    return [refs[order.index(k)] for k in range(len(refs))]


def spread_kernel(rows, scale, inner_scale, place_ref, coeff_ref, *refs):
    spread_ref, spread_t_ref, slope_ref = refs
    experts, bases = coeff_ref.shape
    mix = jnp.tanh(coeff_ref[...])
    slope_ref[...] = (1.0 - mix * mix) * inner_scale
    mix = mix.astype(BF16).astype(F32)
    place = place_ref[0]
    tall = experts * rows
    wide = bases * rows
    owner = jnp.bitwise_xor(iota((tall, bases), 0) // rows, place)
    picked = jnp.zeros((tall, bases), F32)
    for e in range(experts):
        picked = jnp.where(owner == e, mix[e : e + 1, :], picked)
    widen = (iota((bases, wide), 1) // rows == iota((bases, wide), 0)).astype(BF16)
    spread = jnp.dot(picked.astype(BF16), widen, preferred_element_type=F32)
    same = iota((tall, wide), 0) % rows == iota((tall, wide), 1) % rows
    spread = jnp.where(same, spread, 0.0)
    spread_ref[...] = spread.astype(BF16)
    spread_t_ref[...] = (spread.T * scale).astype(BF16)


def streamed(start, source_ref, held_ref, sems):
    step = pl.program_id(0)
    block = held_ref.shape[2]

    def copy(at):
        column = start + at * block
        if not isinstance(column, int):
            column = pl.multiple_of(column, 128)
        return pltpu.make_async_copy(
            source_ref.at[:, pl.ds(column, block)], held_ref.at[at], sems.at[at]
        )

    @pl.when(step == 0)
    def _():
        for at in range(held_ref.shape[0]):
            copy(at).start()

    copy(step).wait()
    return held_ref[step]


def fetch_kernel(start, source_ref, held_ref, token_ref, sems):
    block = held_ref.shape[2]
    copies = [
        pltpu.make_async_copy(
            source_ref.at[:, start + at * block : start + (at + 1) * block],
            held_ref.at[at],
            sems.at[at],
        )
        for at in range(held_ref.shape[0])
    ]
    for copy in copies:
        copy.start()
    token_ref[...] = jnp.zeros_like(token_ref)
    for copy in copies:
        copy.wait()


def mix_kernel(start, spread_ref, bases_ref, *refs):
    *out_refs, held_ref, sems = refs
    held = streamed(start, bases_ref, held_ref, sems)
    mixed = jnp.dot(spread_ref[...], held, preferred_element_type=F32)
    rows = mixed.shape[0] // len(out_refs)
    for j, out_ref in enumerate(out_refs):
        out_ref[...] = mixed[j * rows : (j + 1) * rows].astype(BF16)


def join_kernel(*refs):
    *part_refs, out_ref = refs
    rows = part_refs[0].shape[0]
    for j, part_ref in enumerate(by_place(part_refs)):
        out_ref[j * rows : (j + 1) * rows, :] = part_ref[...]


def fit_kernel(first, start, load_ref, load_t_ref, weights_ref, *refs):
    mixture_refs, refs = refs[:4], refs[4:]
    *refs, held_ref, sems = refs
    weights = streamed(start, weights_ref, held_ref, sems)
    if first:
        near_ref, *far_refs, grad_ref = refs
    else:
        before_ref, near_ref, *far_refs, grad_ref = refs
    mixture = jnp.concatenate([ref[...] for ref in mixture_refs], axis=0)
    product = jnp.dot(load_ref[...], mixture, preferred_element_type=F32)
    residual = (product - weights.astype(F32)).astype(BF16)
    grad = lax.dot_general(
        residual, mixture, (((1,), (1,)), ((), ())), preferred_element_type=F32
    )
    partial = jnp.dot(load_t_ref[...], residual, preferred_element_type=F32)
    half = partial.shape[0] // 2
    near_ref[...] = partial[:half]
    share = half // len(far_refs)
    for j, far_ref in enumerate(far_refs):
        far_ref[...] = partial[half + j * share : half + (j + 1) * share].astype(BF16)

    @pl.when(pl.program_id(0) == 0)
    def _():
        if first:
            grad_ref[...] = grad
        else:
            grad_ref[...] = before_ref[...] + grad

    @pl.when(pl.program_id(0) > 0)
    def _():
        grad_ref[...] += grad


def chip_sum_kernel(near_ref, *refs):
    *got_refs, keep_ref, send_ref = refs
    got = jnp.concatenate([ref[...] for ref in got_refs], axis=0)
    total = near_ref[...] + got.astype(F32)
    half = total.shape[0] // 2
    keep_ref[...] = total[:half]
    send_ref[...] = total[half:].astype(BF16)


def plane_sum_kernel(keep_ref, got_ref, *out_refs):
    total = keep_ref[...] + got_ref[...].astype(F32)
    rows = total.shape[0] // len(out_refs)
    for j, out_ref in enumerate(out_refs):
        out_ref[...] = total[j * rows : (j + 1) * rows].astype(BF16)


def inner_kernel(rows, experts, start, ready, steps, place_ref, bases_ref, *refs):
    if ready:
        ready_ref, *refs = refs
    if ready < steps:
        *refs, held_ref, sems = refs
    *sum_refs, inner_ref, acc_ref = refs
    summed = jnp.concatenate([ref[...] for ref in by_place(sum_refs)], axis=0)
    step = pl.program_id(0)

    def copy(at):
        block = held_ref.shape[2]
        column = start + at * block
        return pltpu.make_async_copy(
            bases_ref.at[:, column : column + block], held_ref.at[at - ready], sems.at[at - ready]
        )

    for at in range(steps):

        @pl.when(step == at)
        def _(at=at):
            if at == 0:
                for later in range(ready, steps):
                    copy(later).start()
            if at < ready:
                held = ready_ref[at]
            else:
                copy(at).wait()
                held = held_ref[at - ready]
            product = lax.dot_general(
                summed, held, (((1,), (1,)), ((), ())), preferred_element_type=F32
            )
            acc_ref[...] = product if at == 0 else acc_ref[...] + product

    @pl.when(pl.program_id(0) == pl.num_programs(0) - 1)
    def _():
        tall, wide = acc_ref.shape
        bases = wide // rows
        same = iota((tall, wide), 0) % rows == iota((tall, wide), 1) % rows
        kept = jnp.where(same, acc_ref[...], 0.0)
        owner = jnp.bitwise_xor(iota((experts, tall), 1) // rows, place_ref[0])
        gather = (owner == iota((experts, tall), 0)).astype(F32)
        narrow = (iota((wide, bases), 0) // rows == iota((wide, bases), 1)).astype(F32)
        by_expert = jnp.dot(gather, kept, precision=HIGHEST, preferred_element_type=F32)
        inner_ref[...] = jnp.dot(
            by_expert, narrow, precision=HIGHEST, preferred_element_type=F32
        )


def basis_kernel(scale, skip, spread_t_ref, *refs):
    *sum_refs, out_ref, token_ref = refs[skip:]
    token_ref[...] = jnp.zeros_like(token_ref)
    summed = jnp.concatenate([ref[...] for ref in by_place(sum_refs)], axis=0)
    grad = jnp.dot(spread_t_ref[...], summed, preferred_element_type=F32)
    if scale != 1.0:
        grad = grad * scale
    out_ref[...] = grad.astype(BF16)


def add_kernel(turns, scaled, *refs):
    *part_refs, out_ref = refs
    if scaled:
        *part_refs, slope_ref = part_refs
    part = {turn: ref[...] for turn, ref in zip((*turns, 0), part_refs)}
    total = part[0] + part[1]
    if len(turns) == 3:
        total = total + (part[2] + part[3])
    out_ref[...] = total * slope_ref[...] if scaled else total


def whole_spec(shape):
    return pl.BlockSpec(shape, lambda s: (0,) * len(shape))


def column_spec(rows, block, start=0):
    return pl.BlockSpec((rows, block), lambda s: (0, start + s))


def per_device(weights, loadings, bases, coeff):
    devices = lax.axis_size("expert")
    num_bases, rows, width = bases.shape
    experts = coeff.shape[0]
    group = devices // experts
    assert group == 4 and experts & (experts - 1) == 0
    ff = loadings.shape[0]
    rank = rows * devices
    tall, wide = experts * rows, num_bases * rows
    split = rows % 16 == 0
    widths = [width * share // sum(SHARES) for share in SHARES] if experts <= 8 else [width]
    chunks = len(widths)
    starts = [sum(widths[:j]) for j in range(chunks)]
    block = math.gcd(*widths)
    while block > LARGE and block % 256 == 0:
        block //= 2
    small = block // 2 if block % 256 == 0 else block
    me = lax.axis_index("expert")
    place = (me // group).astype(jnp.int32).reshape(1)
    smem = pl.BlockSpec(memory_space=pltpu.SMEM)
    vmem = pl.BlockSpec(memory_space=pltpu.VMEM)
    anywhere = pl.BlockSpec(memory_space=pl.ANY)
    hbm = pl.BlockSpec(memory_space=pltpu.HBM)

    def send(x, flip):
        return lax.ppermute(x, "expert", [(i, i ^ flip) for i in range(devices)])

    def send_places(parts):
        sent = {k: send(parts[k], k * group) for k in far_first(experts) if k}
        return [parts[0]] + [sent[k] for k in range(1, experts)]

    def pieces_of(x):
        return [x[j * rows : (j + 1) * rows] for j in range(experts)]

    def pinned(array, spec):
        return pltpu.with_memory_space_constraint(array, pltpu.HBM) if spec is hbm else array

    def call(kernel, name, ins, outs, grid=None, after=(), flops=0, bytes_accessed=0, alias=None, **kw):
        count, late = len(ins), len(after)

        def body(*refs):
            kernel(*refs[:count], *refs[count + late :])

        return pl.pallas_call(
            body,
            out_shape=[shape for shape, _ in outs],
            in_specs=[spec for _, spec in ins] + [anywhere] * late,
            out_specs=[spec for _, spec in outs],
            compiler_params=pltpu.CompilerParams(vmem_limit_bytes=VMEM_LIMIT),
            cost_estimate=pl.CostEstimate(
                flops=flops, bytes_accessed=bytes_accessed, transcendentals=0
            ),
            input_output_aliases=alias or {},
            name=name,
            **({} if grid is None else {"grid": grid}),
            **kw,
        )(*[pinned(array, spec) for array, spec in ins], *after)

    def shape(*dims, dtype=BF16):
        return jax.ShapeDtypeStruct(dims, dtype)

    def col(rows_in, start=0, size=None):
        size = size or block
        return column_spec(rows_in, size, start // size)

    def held(j, rows_in, size, ready=0):
        steps = widths[j] // size - ready
        if not steps:
            return []
        return [pltpu.VMEM((steps, rows_in, size), BF16), pltpu.SemaphoreType.DMA((steps,))]

    flat = bases.reshape(wide, width)
    root = math.isqrt(experts)
    exact = root * root == experts and root & (root - 1) == 0
    spread, spread_t, slope = call(
        functools.partial(
            spread_kernel, rows, 1.0 / root if exact else 1.0, 1.0 / math.sqrt(rank * width)
        ),
        "spread",
        [(place, smem), (coeff, vmem)],
        [
            (shape(tall, wide), vmem),
            (shape(wide, tall), vmem),
            (shape(experts, num_bases, dtype=F32), vmem),
        ],
    )
    late_scale = 1.0 if exact else 1.0 / math.sqrt(experts)

    local = jnp.arange(rank, dtype=jnp.int32)
    piece = local // rows
    flips = (piece % experts) * group + (piece // experts % 2) * 2 + piece // (2 * experts)
    absolute = (me ^ flips) * rows + local % rows
    order = (jnp.arange(rank, dtype=jnp.int32)[:, None] == absolute[None, :]).astype(BF16)
    load = jnp.dot(loadings, order, preferred_element_type=F32).astype(BF16)
    load_t = lax.dot_general(
        order, loadings, (((0,), (1,)), ((), ())), preferred_element_type=F32
    ).astype(BF16)

    def mix_chunk(j, after):
        count = experts if split else 1
        outs = call(
            functools.partial(mix_kernel, starts[j]),
            "mix",
            [(spread, whole_spec((tall, wide))), (flat, hbm)],
            [(shape(tall // count, widths[j]), col(tall // count, 0, small))] * count,
            (widths[j] // small,),
            after,
            FLOPS * 2 * tall * wide * widths[j],
            FLOPS * 2 * wide * widths[j],
            scratch_shapes=held(j, wide, small),
        )
        return list(outs) if split else pieces_of(outs[0])

    def join(j, parts, after):
        if not split:
            return jnp.concatenate(parts, axis=0)
        return call(
            join_kernel,
            "join",
            [(parts[k], vmem) for k in far_first(experts)],
            [(shape(tall, widths[j]), vmem)],
            after=after,
        )[0]

    def far_parts(j):
        return FAR[min(j, len(FAR) - 1)]

    def fetch(j, source, after):
        steps, rows_in = min(READY[j], widths[j] // block), source.shape[0]
        return call(
            functools.partial(fetch_kernel, starts[j]),
            "fetch",
            [(source, hbm)],
            [(shape(steps, rows_in, block), vmem), (shape(8, 128, dtype=F32), vmem)],
            after=after,
            bytes_accessed=FETCH_COST * 4 * rows_in * block * steps,
            scratch_shapes=[pltpu.SemaphoreType.DMA((steps,))],
        )

    def fit_chunk(j, parts, before, after):
        first = before is None
        extra = [] if first else [(before, whole_spec((ff, rank)))]
        half = rank // 2
        return call(
            functools.partial(fit_kernel, first, starts[j]),
            "fit",
            [
                (load, whole_spec((ff, rank))),
                (load_t, whole_spec((rank, ff))),
                (weights, hbm),
                *[(part, col(half // 2)) for part in parts],
                *extra,
            ],
            [
                (shape(half, widths[j], dtype=F32), col(half)),
                *[(shape(half // far_parts(j), widths[j]), col(half // far_parts(j)))] * far_parts(j),
                (shape(ff, rank, dtype=F32), whole_spec((ff, rank))),
            ],
            (widths[j] // block,),
            after,
            FLOPS * 6 * ff * rank * widths[j],
            FLOPS * 2 * ff * widths[j],
            scratch_shapes=held(j, ff, block),
        )

    def chip_sum(j, near, got, after):
        half = rank // 4
        return call(
            chip_sum_kernel,
            "chip_sum",
            [(near, col(2 * half)), *[(part, col(2 * half // len(got))) for part in got]],
            [
                (shape(half, widths[j], dtype=F32), col(half)),
                (shape(half, widths[j]), col(half)),
            ],
            (widths[j] // block,),
            after,
            FLOPS * 2 * half * widths[j],
            FLOPS * 16 * half * widths[j],
        )

    def plane_sum(j, keep, got, after):
        count = experts if split else 1
        outs = call(
            plane_sum_kernel,
            "plane_sum",
            [(keep, col(tall)), (got, col(tall))],
            [(shape(tall // count, widths[j]), col(tall // count))] * count,
            (widths[j] // block,),
            after,
            FLOPS * tall * widths[j],
            FLOPS * 8 * tall * widths[j],
        )
        return list(outs) if split else pieces_of(outs[0])

    def sums_of(sums):
        sums = sums if split else [jnp.concatenate(sums, axis=0)]
        return [(sums[k], col(tall // len(sums))) for k in far_first(len(sums))]

    def inner_chunk(j, sums, after, fetched=None):
        ready = 0 if fetched is None else fetched.shape[0]
        return call(
            functools.partial(inner_kernel, rows, experts, starts[j], ready, widths[j] // block),
            "inner",
            [
                (place, smem),
                (flat, hbm),
                *([(fetched, vmem)] if ready else []),
                *sums_of(sums),
            ],
            [(shape(experts, num_bases, dtype=F32), whole_spec((experts, num_bases)))],
            (widths[j] // block,),
            after,
            FLOPS * 2 * tall * wide * widths[j],
            FLOPS * 2 * wide * widths[j],
            scratch_shapes=[pltpu.VMEM((tall, wide), F32), *held(j, wide, block, ready)],
        )[0]

    def basis_chunk(j, sums, before, after, first=0, last=None):
        extra = [] if before is None else [(before, hbm)]
        unit = block if last is None else small
        last = widths[j] // block if last is None else last
        size = (last - first) * unit
        return call(
            functools.partial(basis_kernel, late_scale, len(extra)),
            "basis",
            [
                (spread_t, whole_spec((wide, tall))),
                *extra,
                *[(part, col(part.shape[0], first * unit, unit)) for part, _ in sums_of(sums)],
            ],
            [
                (shape(wide, width), col(wide, starts[j] + first * unit, unit)),
                (shape(8, 128, dtype=F32), whole_spec((8, 128))),
            ],
            (last - first,),
            after,
            FLOPS * 2 * tall * wide * size,
            FLOPS * 2 * wide * size,
            alias={1: 0} if extra else None,
        )

    mixes, gathered, returned, inners = [], [], [], []
    for j in range(chunks):
        mixes.append(mix_chunk(j, [mixes[-1][0]] if j else []))
    done = [mixes[-1][0]]
    for j in range(chunks):
        mixed = mixes[j]
        got = send_places(mixed)
        own = join(j, got, done)
        done = [own]
        row = send(own, 2)
        gathered.append((own, row, send(own, 1), send(row, 1)))
    grad_local, kept, at_hand = None, {}, {}

    def return_plane(j, after):
        if split and j in FB:
            at_hand[j], token = fetch(j, flat, after)
            after = [token]
        keep, away = kept.pop(j)
        sums = plane_sum(j, keep, away, after)
        returned.append(send_places(sums))
        return [sums[0]]

    for j in range(chunks):
        near, *far, grad_local = fit_chunk(j, gathered[j], grad_local, done)
        done = [near]
        keep, away = chip_sum(j, near, [send(part, 1) for part in far], done)
        kept[j] = keep, send(away, 2)
        done = [keep]
        if j >= LAG:
            done = return_plane(j - LAG, done)
    grad_a = jnp.dot(
        grad_local, order.astype(F32).T, precision=HIGHEST, preferred_element_type=F32
    ) / math.sqrt(width)
    for j in sorted(kept):
        done = return_plane(j, done + [pinned(grad_a, hbm)])
    grad_flat = None
    for j in range(chunks):
        inners.append(inner_chunk(j, returned[j], done, at_hand.get(j)))
        done = [inners[-1]]
        if j < chunks - 1:
            grad_flat, token = basis_chunk(j, returned[j], grad_flat, done)
            done = [token]

    total = sum(inners[1:], inners[0])
    flip, at, blocks = 1, 0, widths[-1] // small
    while flip < devices:
        upto = -(-blocks // 2) if at == 0 else blocks
        turns = P_ORDER if flip * 2 < devices else (1,)
        got = {turn: send(total, turn * flip) for turn in turns}
        flip *= len(turns) + 1
        if at < upto:
            grad_flat, token = basis_chunk(-1, returned[-1], grad_flat, [total], at, upto)
            at = upto
        last = flip >= devices
        total = call(
            functools.partial(add_kernel, turns, last),
            "add",
            [(got[turn], vmem) for turn in turns] + [(total, vmem)] + [(slope, vmem)] * last,
            [(shape(experts, num_bases, dtype=F32), vmem)],
            after=[token],
        )[0]
    return (grad_a, grad_flat.reshape(num_bases, rows, width), total)


def solution(mesh):
    in_specs = (
        P(("layer", "expert"), None),
        P(("layer", "expert"), None),
        P("layer", "expert", None),
        P("layer", None),
    )
    out_specs = (P(("layer", "expert"), None), P("layer", "expert", None), P("layer", None))
    return jax.shard_map(
        per_device, mesh=mesh, in_specs=in_specs, out_specs=out_specs, check_vma=False
    )
```
